32 devices in a mesh: seq: 2 (over x), fsdp: 16 (over z, y, core).
Axes of the slice: x: 2, y: 2, z: 4, core: 2. Of those that a mesh axis runs over, the one named last changes fastest.
Arguments:
- tokens: bfloat16 [16, 256, 768], P('fsdp', 'seq'), may hold values from -4 to 4
- cond: bfloat16 [16, 768], P('fsdp'), may hold values from -2.5 to 2.5
- w_ada: bfloat16 [768, 4608], P(('seq', 'fsdp')), may hold values from -0.21875 to 0.21875
- b_ada: bfloat16 [4608], P(('seq', 'fsdp')), may hold values from -1 to 1
- w_qkv: bfloat16 [768, 2304], P(('seq', 'fsdp')), may hold values from -0.3125 to 0.3125
- b_query: bfloat16 [768], P(('seq', 'fsdp')), may hold values from -1.5 to 1.5
- b_value: bfloat16 [768], P(('seq', 'fsdp')), may hold values from -1.5 to 1.5
- w_proj: bfloat16 [768, 768], P(('seq', 'fsdp')), may hold values from -0.875 to 0.875
- b_proj: bfloat16 [768], P(('seq', 'fsdp')), may hold values from -1.5 to 1.5
- w_fc1: bfloat16 [768, 3072], P(('seq', 'fsdp')), may hold values from -0.21875 to 0.21875
- b_fc1: bfloat16 [3072], P(('seq', 'fsdp')), may hold values from -1.5 to 1.5
- w_fc2: bfloat16 [3072, 768], P(('seq', 'fsdp')), may hold values from -0.15625 to 0.15625
- b_fc2: bfloat16 [768], P(('seq', 'fsdp')), may hold values from -1.5 to 1.5
- cotangent: bfloat16 [16, 256, 768], P('fsdp', 'seq'), may hold values from -4 to 4
Outputs:
- output: bfloat16 [16, 256, 768], P('fsdp', 'seq')
- grad_tokens: bfloat16 [16, 256, 768], P('fsdp', 'seq')
- grad_cond: bfloat16 [16, 768], P('fsdp')
- grad_w_ada: float32 [768, 4608], P(('seq', 'fsdp'))
- grad_b_ada: float32 [4608], P(('seq', 'fsdp'))
- grad_w_qkv: float32 [768, 2304], P(('seq', 'fsdp'))
- grad_b_query: float32 [768], P(('seq', 'fsdp'))
- grad_b_value: float32 [768], P(('seq', 'fsdp'))
- grad_w_proj: float32 [768, 768], P(('seq', 'fsdp'))
- grad_b_proj: float32 [768], P(('seq', 'fsdp'))
- grad_w_fc1: float32 [768, 3072], P(('seq', 'fsdp'))
- grad_b_fc1: float32 [3072], P(('seq', 'fsdp'))
- grad_w_fc2: float32 [3072, 768], P(('seq', 'fsdp'))
- grad_b_fc2: float32 [768], P(('seq', 'fsdp'))
The draws below stay inside these ranges and needn't reach their ends.
All inputs are finite; a program needn't handle non-finite values.
Results may differ from the reference program's by a relative error of at most 0.017.
The reference program's roundings to bfloat16 on the way count: a program that leaves them out, or rounds other values in their place, can miss the bound.
Values may be sent and summed in bfloat16 or wider, within the bound.
No kernel may reach another device: no remote copies, remote signals or barrier semaphores. Data moves between devices by JAX's collectives and lax.ppermute only.
A program may use at most 256 MiB of HBM per device.

```python
import math
import jax
import jax.numpy as jnp
from jax import lax

D = 768
H = 12
HD = 64
FF = 3072
SEQ_LEN = 256
LAT = 16


def block_levels(stream_key, shape, cuts, least, high):
    factor_of, own = 1.0, jax.random.fold_in(stream_key, 6)
    for axis_at, blocks in cuts:
        heights = jnp.exp(jax.random.uniform(jax.random.fold_in(own, axis_at), (blocks,), jnp.float32, least / len(cuts), high / len(cuts)))
        factor_of = factor_of * jnp.repeat(heights, shape[axis_at] // blocks).reshape([-1 if axis == axis_at else 1 for axis in range(len(shape))])
    return factor_of


def gaussian(stream_key, dims, scale, most, split=(), held_as=jnp.bfloat16):
    entries = jax.random.normal(stream_key, dims, jnp.float32) * scale
    if len(split) > 0:
        entries = block_levels(stream_key, dims, split, -0.22, 0.18) * entries
    return jnp.clip(entries, min=-most, max=most).astype(held_as)


def setup_inputs(seed: int = 0) -> dict:
    streams_of = jax.random.split(jax.random.key(seed), 15)
    return {
        "tokens": gaussian(streams_of[0], (LAT, SEQ_LEN, D), 1.0, 4.0, ((0, 16), (1, 2))),
        "cond": gaussian(streams_of[1], (LAT, D), 1.0, 2.5, ((0, 16),)),
        "w_ada": gaussian(streams_of[2], (D, 6 * D), D ** -0.5, 0.21875, ((0, 32),)),
        "b_ada": gaussian(streams_of[3], (6 * D,), 0.3, 1.0, ((0, 32),)),
        "w_qkv": gaussian(streams_of[4], (D, 3 * D), (D // 2) ** -0.5, 0.3125, ((0, 32),)),
        "b_query": gaussian(streams_of[5], (D,), 0.5, 1.5, ((0, 32),)),
        "b_value": gaussian(streams_of[6], (D,), 0.5, 1.5, ((0, 32),)),
        "w_proj": gaussian(streams_of[7], (D, D), (D // 16) ** -0.5, 0.875, ((0, 32),)),
        "b_proj": gaussian(streams_of[8], (D,), 0.5, 1.5, ((0, 32),)),
        "w_fc1": gaussian(streams_of[9], (D, FF), D ** -0.5, 0.21875, ((0, 32),)),
        "b_fc1": gaussian(streams_of[10], (FF,), 0.5, 1.5, ((0, 32),)),
        "w_fc2": gaussian(streams_of[11], (FF, D), (FF // 2) ** -0.5, 0.15625, ((0, 32),)),
        "b_fc2": gaussian(streams_of[12], (D,), 0.5, 1.5, ((0, 32),)),
        "cotangent": gaussian(streams_of[13], (LAT, SEQ_LEN, D), 1.0, 4.0, ((0, 16), (1, 2))),
    }


@jax.custom_vjp
def low(v):
    return lax.optimization_barrier(v.astype(jnp.bfloat16)).astype(jnp.float32)

@jax.custom_vjp
def low_back(v):
    return v

def low_keep(v):
    return (low(v), None)

def low_pass(kept, grad):
    return (grad,)

def back_keep(v):
    return (v, None)

def back_low(kept, grad):
    return (low(grad),)
low.defvjp(low_keep, low_pass)
low_back.defvjp(back_keep, back_low)

def both_ways(value):
    return low_back(low(value))

def dot_high(left, right):
    return jnp.dot(left, right, precision=lax.Precision.HIGHEST, preferred_element_type=jnp.float32)

def normalize(value):
    centre = value - lax.optimization_barrier(jnp.mean(value, axis=-1, keepdims=True))
    variance = lax.optimization_barrier(jnp.mean(centre * centre, axis=-1, keepdims=True))
    return centre * lax.rsqrt(variance + 1e-06)

def gelu_tanh(value):
    return 0.5 * value * (1.0 + jnp.tanh(0.7978845608028654 * (value + 0.044715 * value * value * value)))

def layer_group(block, weights):
    x_group, mod_group = block
    w_qkv, b_query, b_value, w_proj, b_proj, w_fc1, b_fc1, w_fc2, b_fc2 = weights
    count = x_group.shape[0]
    parts = [mod_group[:, None, index * D:(index + 1) * D] for index in range(6)]
    shift_attn, scale_attn, gate_attn, shift_mlp, scale_mlp, gate_mlp = parts
    h_attn = low(normalize(x_group) * (1.0 + scale_attn) + shift_attn)
    bias_qkv = jnp.concatenate([b_query, jnp.zeros_like(b_query), b_value])
    qkv = both_ways(dot_high(h_attn, w_qkv) + bias_qkv)
    query = qkv[..., :D].reshape(count, SEQ_LEN, H, HD)
    key = qkv[..., D:2 * D].reshape(count, SEQ_LEN, H, HD)
    value = qkv[..., 2 * D:].reshape(count, SEQ_LEN, H, HD)
    scores = jnp.einsum('gqhd,gkhd->ghqk', query, key, precision=lax.Precision.HIGHEST)
    scores = low_back(scores * HD ** (-0.5))
    probs = low(jax.nn.softmax(scores, axis=-1))
    attended = jnp.einsum('ghqk,gkhd->gqhd', probs, value, precision=lax.Precision.HIGHEST)
    attended = both_ways(attended.reshape(count, SEQ_LEN, D))
    attn = low_back(dot_high(attended, w_proj) + b_proj)
    mid = x_group + gate_attn * attn
    perceptron_input = low(normalize(mid) * (1.0 + scale_mlp) + shift_mlp)
    up_value = low_back(dot_high(perceptron_input, w_fc1) + b_fc1)
    activated_hidden = low(gelu_tanh(up_value))
    branch = low_back(dot_high(activated_hidden, w_fc2) + b_fc2)
    return mid + gate_mlp * branch

def forward(tokens, cond, w_ada, b_ada, w_qkv, b_query, b_value, w_proj, b_proj, w_fc1, b_fc1, w_fc2, b_fc2):
    modulation = low_back(dot_high(low(jax.nn.silu(cond)), w_ada) + b_ada)
    group = math.gcd(LAT, 16)
    blocks = LAT // group
    x_blocks = tokens.reshape(blocks, group, SEQ_LEN, D)
    mod_blocks = modulation.reshape(blocks, group, 6 * D)
    weights = (w_qkv, b_query, b_value, w_proj, b_proj, w_fc1, b_fc1, w_fc2, b_fc2)

    def one_block(block):
        return layer_group(block, weights)
    result = lax.map(jax.checkpoint(one_block), (x_blocks, mod_blocks))
    return result.reshape(LAT, SEQ_LEN, D)

def reference(tokens, cond, w_ada, b_ada, w_qkv, b_query, b_value, w_proj, b_proj, w_fc1, b_fc1, w_fc2, b_fc2, cotangent):
    inputs = [arr.astype(jnp.float32) for arr in (tokens, cond, w_ada, b_ada, w_qkv, b_query, b_value, w_proj, b_proj, w_fc1, b_fc1, w_fc2, b_fc2)]
    result, pullback = jax.vjp(forward, *inputs)
    grads = pullback(cotangent.astype(jnp.float32))
    return (result.astype(jnp.bfloat16), grads[0].astype(jnp.bfloat16), grads[1].astype(jnp.bfloat16), grads[2], grads[3], grads[4], grads[5], grads[6], grads[7], grads[8], grads[9], grads[10], grads[11], grads[12])
```

```python
import math

import jax
import jax.numpy as jnp
from jax import lax
from jax.sharding import PartitionSpec as P

HD = 64
AXES = ("seq", "fsdp")
F32 = jnp.float32
BF16 = jnp.bfloat16


def normalize(value):
    centre = value - jnp.mean(value, axis=-1, keepdims=True)
    variance = jnp.mean(centre * centre, axis=-1, keepdims=True)
    return centre * lax.rsqrt(variance + 1e-06)


def modulate(value, shift, scale):
    return normalize(value) * (1.0 + scale) + shift


def gelu_tanh(value):
    return (
        0.5
        * value
        * (1.0 + jnp.tanh(0.7978845608028654 * (value + 0.044715 * value * value * value)))
    )


def dot(left, right):
    return jnp.dot(left, right, preferred_element_type=F32)


def dot_rt(left, right):
    return lax.dot_general(left, right, (((1,), (1,)), ((), ())), preferred_element_type=F32)


def dot_lt(left, right):
    return lax.dot_general(left, right, (((0,), (0,)), ((), ())), preferred_element_type=F32)


class Links:
    def __init__(self, devices):
        self.devices = devices
        self.index = lax.axis_index(AXES)

    def place(self, bits):
        spot = jnp.int32(0)
        for bit in bits:
            spot = spot * 2 + ((self.index >> bit) & 1)
        return spot

    def mask(self, bits, step):
        total = 0
        for at, bit in enumerate(reversed(bits)):
            total |= ((step >> at) & 1) << bit
        return total

    def send(self, value, bits, step=1):
        mask = self.mask(bits, step)
        return lax.ppermute(value, AXES, [(i, i ^ mask) for i in range(self.devices)])

    def gather(self, value, bits, axis):
        count = 1 << len(bits)
        spot = self.place(bits)
        arrived = [value] + [self.send(value, bits, step) for step in range(1, count)]
        if count == 2:
            first = jnp.stack(arrived, axis)
            second = jnp.stack(arrived[::-1], axis)
            return jnp.where(spot == 0, first, second)
        shape = value.shape[:axis] + (count,) + value.shape[axis:]
        out = jnp.zeros(shape, value.dtype)
        for step, part in enumerate(arrived):
            out = lax.dynamic_update_index_in_dim(out, part, spot ^ step, axis)
        return out

    def pick(self, value, spot, axis=0):
        return lax.dynamic_index_in_dim(value, spot, axis, keepdims=False)

    def exchange(self, value, bits):
        spot = self.place(bits)
        out = value
        for step in range(1, 1 << len(bits)):
            part = self.send(self.pick(value, spot ^ step), bits, step)
            out = lax.dynamic_update_index_in_dim(out, part, spot ^ step, 0)
        return out

    def scatter(self, value, bits, axis):
        spot = self.place(bits)
        total = self.pick(value, spot, axis).astype(F32)
        for step in range(1, 1 << len(bits)):
            part = self.pick(value, spot ^ step, axis).astype(BF16)
            total = total + self.send(part, bits, step).astype(F32)
        return total


def bit_groups(bits):
    high = list(reversed(bits))
    return [high[at : at + 2] for at in range(0, len(high), 2)]


def local(
    shards,
    split,
    tokens,
    cond,
    w_ada,
    b_ada,
    w_qkv,
    b_query,
    b_value,
    w_proj,
    b_proj,
    w_fc1,
    b_fc1,
    w_fc2,
    b_fc2,
    cotangent,
):
    seq, fsdp = split
    link = Links(shards)
    low_bits = int(math.log2(fsdp))
    core_bit = [0]
    seq_bits = list(range(low_bits, int(math.log2(shards))))[::-1]
    rest_bits = list(range(1, low_bits))
    rest = fsdp // 2
    team = seq * 2
    team_bits = seq_bits + core_bit
    core = link.place(core_bit)
    half = link.place(seq_bits)
    me = link.place(team_bits)
    latents, local_len, width = tokens.shape
    seq_len = seq * local_len
    rows = w_qkv.shape[0]
    hidden_rows = w_fc2.shape[0]
    hidden = hidden_rows * rest
    group = width // team
    heads = group // HD
    count = 2 * latents

    def gather_rest(value):
        first, last = value.shape[0], value.shape[1:]
        value = value[:, None]
        for bits in bit_groups(rest_bits):
            value = link.gather(value, bits, 2)
            value = value.reshape((first, -1) + last)
        return value

    def scatter_rest(value):
        first, last = value.shape[0], value.shape[2:]
        for bits in bit_groups(rest_bits)[::-1]:
            value = value.reshape((first, -1, 1 << len(bits)) + last)
            value = link.scatter(value, bits, 2)
        return value[:, 0]

    def both_halves(value):
        value = link.gather(value, seq_bits, 1).reshape(latents, seq_len, -1)
        return link.gather(value, core_bit, 0).reshape(count, seq_len, -1)

    cond_float = cond.astype(F32)
    silu_cond = jax.nn.silu(cond_float).astype(BF16)
    cond_blocks = silu_cond.reshape(latents, shards, rows).swapaxes(0, 1).reshape(shards, -1)
    small = jnp.concatenate([b_query, b_value, b_proj, b_fc2, b_fc1])
    small = jnp.concatenate(
        [cond_blocks, jnp.broadcast_to(small, (shards, small.shape[0]))], axis=1
    )
    small = lax.all_to_all(small, AXES, 0, 0, tiled=True)
    mine = latents * rows
    all_cond = small[:fsdp, :mine].reshape(fsdp * latents, rows)
    full_query = small[:, mine : mine + rows].reshape(-1)
    full_value = small[:, mine + rows : mine + 2 * rows].reshape(-1)
    bias_proj = small[:, mine + 2 * rows : mine + 3 * rows].reshape(-1).astype(F32)
    bias_fc2 = small[:, mine + 3 * rows : mine + 4 * rows].reshape(-1).astype(F32)
    bias_fc1 = small[:, mine + 4 * rows :].reshape(seq, rest, 2, hidden_rows)
    bias_fc1 = link.pick(link.pick(bias_fc1, half, 0), core, 1).reshape(-1).astype(F32)

    team_qkv = w_qkv.reshape(rows, 3, team, group).transpose(2, 0, 1, 3)
    team_qkv = link.exchange(team_qkv.reshape(team, rows, 3 * group), team_bits)
    my_qkv = gather_rest(team_qkv.reshape(seq, 2 * rows, 3 * group)).reshape(width, 3 * group)
    full_proj = gather_rest(w_proj[None])[0]
    full_proj = link.gather(full_proj, seq_bits, 0)
    full_proj = link.gather(full_proj, core_bit, 2).reshape(width, width)
    team_fc1 = w_fc1.reshape(rows, seq, rest, 2, hidden_rows).transpose(1, 3, 0, 2, 4)
    team_fc1 = link.exchange(team_fc1.reshape(team, rows, hidden), team_bits)
    my_fc1 = gather_rest(team_fc1.reshape(seq, 2 * rows, hidden)).reshape(width, hidden)
    my_fc2 = gather_rest(w_fc2[None]).reshape(hidden, width)
    all_tokens = both_halves(tokens).astype(F32)
    all_cotangent = both_halves(cotangent).astype(F32)

    part = dot(all_cond, w_ada)
    own_columns = (jnp.arange(shards) == link.index)[:, None] * b_ada.astype(F32)[None, :]
    part = part + own_columns.reshape(-1)
    part = part.reshape(1, fsdp, latents * 6 * width)
    part = jnp.broadcast_to(part, (seq, fsdp, latents * 6 * width)).reshape(shards, -1)
    part = lax.all_to_all(part, AXES, 0, 0, tiled=True)
    modulation = jnp.sum(part, axis=0).reshape(latents, 1, 6 * width)
    modulation = link.gather(modulation, core_bit, 0).reshape(count, 1, 6 * width)
    parts = [modulation[..., at * width : (at + 1) * width] for at in range(6)]
    shift_attn, scale_attn, gate_attn, shift_mlp, scale_mlp, gate_mlp = parts

    def own(value):
        return lax.dynamic_slice_in_dim(value, core * latents, latents, 0)

    def own_rows(value):
        return lax.dynamic_slice_in_dim(value, half * local_len, local_len, 1)

    def sum_team(value):
        value = link.scatter(value.reshape(2, latents, seq_len, width), core_bit, 0)
        value = value.astype(BF16)
        return value.astype(F32) + link.send(value, seq_bits).astype(F32)

    def flat(value):
        return value.reshape(count * seq_len, -1)

    h_attn = modulate(all_tokens, shift_attn, scale_attn).astype(BF16)
    bias_q = lax.dynamic_slice_in_dim(full_query, me * group, group, 0)
    bias_v = lax.dynamic_slice_in_dim(full_value, me * group, group, 0)
    bias_qkv = jnp.concatenate([bias_q, jnp.zeros_like(bias_q), bias_v]).astype(F32)
    qkv = (dot(flat(h_attn), my_qkv) + bias_qkv).astype(BF16)
    qkv = qkv.reshape(count, seq_len, 3, heads, HD)
    query, key, value = qkv[:, :, 0], qkv[:, :, 1], qkv[:, :, 2]
    scores = jnp.einsum("lqhd,lkhd->lhqk", query, key, preferred_element_type=F32) * HD ** (-0.5)
    top = jnp.max(scores, axis=-1, keepdims=True)
    log_total = top + jnp.log(jnp.sum(jnp.exp(scores - top), axis=-1, keepdims=True))
    probs = jnp.exp(scores - log_total)
    probs_low = probs.astype(BF16)
    attended = jnp.einsum("lhqk,lkhd->lqhd", probs_low, value, preferred_element_type=F32)
    attended = attended.astype(BF16).reshape(count * seq_len, group)
    all_attended = link.gather(link.gather(attended, seq_bits, 0), core_bit, 1)
    all_attended = all_attended.reshape(team, count * seq_len, group)
    attn = jnp.einsum(
        "tnd,tde->ne",
        all_attended,
        full_proj.reshape(team, group, width),
        preferred_element_type=F32,
    )
    attn = (attn + bias_proj).reshape(count, seq_len, width)
    mid = all_tokens + gate_attn * attn

    h_mlp = flat(modulate(mid, shift_mlp, scale_mlp).astype(BF16))
    up = dot(h_mlp, my_fc1) + bias_fc1
    activated, gelu_back = jax.vjp(gelu_tanh, up)
    activated = activated.astype(BF16)
    grad_branch = flat((gate_mlp * all_cotangent).astype(BF16))
    grad_up = gelu_back(dot_rt(grad_branch, my_fc2))[0].astype(BF16)
    grad_h_mlp = sum_team(dot_rt(grad_up, my_fc1).reshape(count, seq_len, width))

    own_tokens = own(all_tokens)
    own_cotangent = own(all_cotangent)
    own_mid = own(mid)
    mlp_back = jax.vjp(modulate, own_mid, own(shift_mlp), own(scale_mlp))[1]
    grad_mid, grad_shift_mlp, grad_scale_mlp = mlp_back(grad_h_mlp)
    grad_mid = grad_mid + own_cotangent
    grad_gate_attn = jnp.sum(grad_mid * own(attn), axis=1, keepdims=True)
    grad_attn = (own(gate_attn) * grad_mid).astype(BF16)
    grad_attn = link.gather(grad_attn, core_bit, 0).reshape(count * seq_len, width)

    grad_fc2 = dot_lt(activated, grad_branch).astype(BF16)
    grad_fc2 = scatter_rest(grad_fc2.reshape(1, rest, hidden_rows, width))[0]
    grad_fc1 = dot_lt(h_mlp, grad_up).astype(BF16)
    grad_fc1 = scatter_rest(grad_fc1.reshape(seq, rest, 2 * rows, hidden)).astype(BF16)
    grad_fc1 = link.exchange(grad_fc1.reshape(team, rows, hidden), team_bits)
    grad_fc1 = grad_fc1.reshape(seq, 2, rows, rest, hidden_rows).transpose(2, 0, 3, 1, 4)
    grad_fc1 = grad_fc1.reshape(rows, -1).astype(F32)

    branch = dot(activated, my_fc2).reshape(2, latents, seq_len, width)
    branch = link.scatter(branch, core_bit, 0).reshape(latents, seq, local_len, width)
    branch = link.scatter(branch, seq_bits, 1) + bias_fc2
    output = (own_rows(own_mid) + own(gate_mlp) * branch).astype(BF16)
    grad_gate_mlp = jnp.sum(cotangent.astype(F32) * branch, axis=1, keepdims=True)
    grad_gate_mlp = grad_gate_mlp + link.send(grad_gate_mlp, seq_bits)

    my_proj = lax.dynamic_slice_in_dim(full_proj, me * group, group, 0)
    grad_heads = dot_rt(grad_attn, my_proj).astype(BF16).reshape(count, seq_len, heads, HD)
    grad_probs = jnp.einsum("lqhd,lkhd->lhqk", grad_heads, value, preferred_element_type=F32)
    row_sums = jnp.sum(grad_probs * probs, axis=-1, keepdims=True)
    grad_scores = (probs * (grad_probs - row_sums)).astype(BF16)
    grad_value = jnp.einsum(
        "lhqk,lqhd->lkhd", probs_low, grad_heads, preferred_element_type=F32
    ).astype(BF16)
    grad_query = (
        jnp.einsum("lhqk,lkhd->lqhd", grad_scores, key, preferred_element_type=F32) * HD ** (-0.5)
    ).astype(BF16)
    grad_key = (
        jnp.einsum("lhqk,lqhd->lkhd", grad_scores, query, preferred_element_type=F32)
        * HD ** (-0.5)
    ).astype(BF16)
    grad_qkv = jnp.stack([grad_query, grad_key, grad_value], axis=2)
    grad_qkv = grad_qkv.reshape(count * seq_len, 3 * group)
    grad_h_attn = sum_team(dot_rt(grad_qkv, my_qkv).reshape(count, seq_len, width))
    grad_w_qkv = dot_lt(flat(h_attn), grad_qkv).astype(BF16)
    grad_w_qkv = scatter_rest(grad_w_qkv.reshape(seq, rest, 2 * rows, 3 * group)).astype(BF16)
    grad_w_qkv = link.exchange(grad_w_qkv.reshape(team, rows, 3 * group), team_bits)
    grad_w_qkv = grad_w_qkv.reshape(team, rows, 3, group).transpose(1, 2, 0, 3)
    grad_w_qkv = grad_w_qkv.reshape(rows, -1).astype(F32)

    grad_proj = dot_lt(attended, grad_attn).astype(BF16)
    grad_proj = grad_proj.reshape(rest // 2, 2, rows, width).swapaxes(0, 1)
    grad_proj = link.exchange(grad_proj, core_bit).reshape(1, rest, rows, width)
    grad_proj = scatter_rest(grad_proj)[0]

    attn_back = jax.vjp(modulate, own_tokens, own(shift_attn), own(scale_attn))[1]
    grad_res, grad_shift_attn, grad_scale_attn = attn_back(grad_h_attn)
    grad_tokens = own_rows(grad_mid + grad_res).astype(BF16)

    grad_mod = jnp.concatenate(
        [
            grad_shift_attn,
            grad_scale_attn,
            grad_gate_attn,
            grad_shift_mlp,
            grad_scale_mlp,
            grad_gate_mlp,
        ],
        axis=-1,
    ).astype(BF16)
    grad_mod = gather_rest(grad_mod.reshape(1, latents, 6 * width))[0]
    grad_mod = link.gather(grad_mod, core_bit, 1).reshape(fsdp * latents, 6 * width)
    grad_ada = dot_lt(all_cond, grad_mod)
    own_ada = b_ada.shape[0]
    grad_b_ada = lax.dynamic_slice_in_dim(grad_mod, link.index * own_ada, own_ada, 1)
    grad_b_ada = jnp.sum(grad_b_ada.astype(F32), axis=0)
    grad_silu = dot_rt(grad_mod, w_ada).reshape(1, fsdp, latents * rows)
    grad_silu = jnp.broadcast_to(grad_silu, (seq, fsdp, latents * rows)).reshape(shards, -1)

    def column_sums(value):
        return jnp.sum(value.astype(F32), axis=0)

    everyone = 1.0 / team
    by_owner = [
        (column_sums(grad_branch) * everyone).reshape(shards, rows),
        (column_sums(grad_attn) * everyone).reshape(shards, rows),
    ]
    sums_qkv = column_sums(grad_qkv)
    in_team = (jnp.arange(team) == me)[:, None]
    for sums in (sums_qkv[:group], sums_qkv[2 * group :]):
        by_owner.append(jnp.where(in_team, sums[None, :], 0.0).reshape(shards, rows))
    sums_up = column_sums(grad_up).reshape(1, rest, 1, hidden_rows)
    in_seq = jnp.arange(seq).reshape(seq, 1, 1, 1) == half
    in_core = jnp.arange(2).reshape(1, 1, 2, 1) == core
    by_owner.append(jnp.where(in_seq & in_core, sums_up, 0.0).reshape(shards, hidden_rows))
    tail = jnp.concatenate([grad_silu] + by_owner, axis=1)
    tail = lax.all_to_all(tail, AXES, 0, 0, tiled=True)
    grad_silu = tail[:, :mine].reshape(shards, latents, rows).swapaxes(0, 1)
    grad_silu = grad_silu.reshape(latents, width)
    silu_back = jax.vjp(jax.nn.silu, cond_float)[1]
    grad_cond = silu_back(grad_silu)[0].astype(BF16)
    sums = jnp.sum(tail[:, mine:], axis=0)
    return (
        output,
        grad_tokens,
        grad_cond,
        grad_ada,
        grad_b_ada,
        grad_w_qkv,
        sums[2 * rows : 3 * rows],
        sums[3 * rows : 4 * rows],
        grad_proj,
        sums[rows : 2 * rows],
        grad_fc1,
        sums[4 * rows :],
        grad_fc2,
        sums[:rows],
    )


def solution(mesh):
    seq, fsdp = mesh.shape["seq"], mesh.shape["fsdp"]
    act = P("fsdp", "seq", None)
    matrix = P(AXES, None)
    vector = P(AXES)
    cond = P("fsdp", None)
    in_specs = (
        act, cond, matrix, vector, matrix, vector, vector, matrix, vector, matrix, vector, matrix,
        vector, act,
    )
    out_specs = (
        act, act, cond, matrix, vector, matrix, vector, vector, matrix, vector, matrix, vector,
        matrix, vector,
    )

    def layer(*args):
        return local(seq * fsdp, (seq, fsdp), *args)

    return jax.shard_map(layer, mesh=mesh, in_specs=in_specs, out_specs=out_specs, check_vma=False)
```

```python
import math

import jax
import jax.numpy as jnp
from jax import lax
from jax.sharding import PartitionSpec as P

HD = 64
AXES = ("seq", "fsdp")
F32 = jnp.float32
BF16 = jnp.bfloat16


def normalize(value):
    centre = value - jnp.mean(value, axis=-1, keepdims=True)
    variance = jnp.mean(centre * centre, axis=-1, keepdims=True)
    return centre * lax.rsqrt(variance + 1e-06)


def modulate(value, shift, scale):
    return normalize(value) * (1.0 + scale) + shift


def gelu_tanh(value):
    return (
        0.5
        * value
        * (1.0 + jnp.tanh(0.7978845608028654 * (value + 0.044715 * value * value * value)))
    )


def dot(left, right):
    return jnp.dot(left, right, preferred_element_type=F32)


def dot_rt(left, right):
    return lax.dot_general(left, right, (((1,), (1,)), ((), ())), preferred_element_type=F32)


def dot_lt(left, right):
    return lax.dot_general(left, right, (((0,), (0,)), ((), ())), preferred_element_type=F32)


def after(value, *earlier):
    return lax.optimization_barrier((value,) + earlier)[0]


class Links:
    def __init__(self, devices):
        self.devices = devices
        self.index = lax.axis_index(AXES)

    def place(self, bits):
        spot = jnp.int32(0)
        for bit in bits:
            spot = spot * 2 + ((self.index >> bit) & 1)
        return spot

    def mask(self, bits, step):
        total = 0
        for at, bit in enumerate(reversed(bits)):
            total |= ((step >> at) & 1) << bit
        return total

    def send(self, value, bits, step=1):
        mask = self.mask(bits, step)
        return lax.ppermute(value, AXES, [(i, i ^ mask) for i in range(self.devices)])

    def own_first(self, value, bits, axis):
        arrived = [value] + [self.send(value, bits, step) for step in range(1, 1 << len(bits))]
        return jnp.stack(arrived, axis)

    def gather(self, value, bits, axis):
        count = 1 << len(bits)
        spot = self.place(bits)
        arrived = [value] + [self.send(value, bits, step) for step in range(1, count)]
        if count == 2:
            first = jnp.stack(arrived, axis)
            second = jnp.stack(arrived[::-1], axis)
            return jnp.where(spot == 0, first, second)
        shape = value.shape[:axis] + (count,) + value.shape[axis:]
        out = jnp.zeros(shape, value.dtype)
        for step, part in enumerate(arrived):
            out = lax.dynamic_update_index_in_dim(out, part, spot ^ step, axis)
        return out

    def pick(self, value, spot, axis=0):
        return lax.dynamic_index_in_dim(value, spot, axis, keepdims=False)

    def exchange(self, value, bits):
        spot = self.place(bits)
        out = value
        for step in range(1, 1 << len(bits)):
            part = self.send(self.pick(value, spot ^ step), bits, step)
            out = lax.dynamic_update_index_in_dim(out, part, spot ^ step, 0)
        return out

    def scatter(self, value, bits, axis, earlier=()):
        spot = self.place(bits)
        arrived = []
        for step in range(1, 1 << len(bits)):
            part = self.pick(value, spot ^ step, axis).astype(BF16)
            arrived.append(self.send(part, bits, step))
        total = self.pick(value, spot, axis)
        if earlier:
            total = after(total, *earlier)
        total = total.astype(F32)
        for part in arrived:
            total = total + part.astype(F32)
        return total


def bit_groups(bits):
    high = list(reversed(bits))
    return [high[at : at + 2] for at in range(0, len(high), 2)]


def local(
    shards,
    split,
    tokens,
    cond,
    w_ada,
    b_ada,
    w_qkv,
    b_query,
    b_value,
    w_proj,
    b_proj,
    w_fc1,
    b_fc1,
    w_fc2,
    b_fc2,
    cotangent,
):
    seq, fsdp = split
    link = Links(shards)
    low_bits = int(math.log2(fsdp))
    core_bit = [0]
    seq_bits = list(range(low_bits, int(math.log2(shards))))[::-1]
    rest_bits = list(range(1, low_bits))
    rest = fsdp // 2
    team = seq * 2
    team_bits = seq_bits + core_bit
    core = link.place(core_bit)
    half = link.place(seq_bits)
    me = link.place(team_bits)
    latents, local_len, width = tokens.shape
    seq_len = seq * local_len
    rows = w_qkv.shape[0]
    hidden_rows = w_fc2.shape[0]
    hidden = hidden_rows * rest
    group = width // team
    heads = group // HD
    count = 2 * latents
    own_flat = latents * seq_len

    def gather_rest(value, earlier=()):
        first, last = value.shape[0], value.shape[1:]
        value = value[:, None]
        if earlier:
            value = after(value, *earlier)
        begun = None
        for bits in bit_groups(rest_bits):
            value = link.gather(value, bits, 2)
            value = value.reshape((first, -1) + last)
            begun = value if begun is None else begun
        return value, begun

    def scatter_rest(value, earlier=()):
        first, last = value.shape[0], value.shape[2:]
        for at, bits in enumerate(bit_groups(rest_bits)[::-1]):
            value = value.reshape((first, -1, 1 << len(bits)) + last)
            value = link.scatter(value, bits, 2, earlier[at] if at < len(earlier) else ())
        return value[:, 0]

    def all_rest(value):
        for bits in bit_groups(rest_bits) + [core_bit]:
            lead = value.shape[:-2]
            value = link.own_first(value, bits, len(lead))
            value = value.reshape((-1,) + value.shape[-2:])
        there = link.index % fsdp ^ jnp.arange(fsdp)
        order = (jnp.arange(fsdp)[:, None] == there[None, :]).astype(value.dtype)
        value = dot(order, value.reshape(fsdp, -1)).astype(value.dtype)
        return value.reshape(fsdp * latents, -1)

    def halves(value):
        return link.gather(value, seq_bits, 1).reshape(latents, seq_len, -1)

    def cores(value):
        return link.own_first(value, core_bit, 0).reshape((count,) + value.shape[1:])

    cond_float = cond.astype(F32)
    silu_cond = jax.nn.silu(cond_float).astype(BF16)
    cond_blocks = silu_cond.reshape(latents, shards, rows).swapaxes(0, 1).reshape(shards, -1)
    small = jnp.concatenate([b_query, b_value, b_proj, b_fc2, b_fc1])
    small = jnp.concatenate(
        [cond_blocks, jnp.broadcast_to(small, (shards, small.shape[0]))], axis=1
    )
    small = lax.all_to_all(small, AXES, 0, 0, tiled=True)
    mine = latents * rows
    all_cond = small[:fsdp, :mine].reshape(fsdp * latents, rows)
    full_query = small[:, mine : mine + rows].reshape(-1)
    full_value = small[:, mine + rows : mine + 2 * rows].reshape(-1)
    bias_proj = small[:, mine + 2 * rows : mine + 3 * rows].reshape(-1).astype(F32)
    bias_fc2 = small[:, mine + 3 * rows : mine + 4 * rows].reshape(-1).astype(F32)
    bias_fc1 = small[:, mine + 4 * rows :].reshape(seq, rest, 2, hidden_rows)
    bias_fc1 = link.pick(link.pick(bias_fc1, half, 0), core, 1).reshape(-1).astype(F32)

    part = dot(all_cond, w_ada)
    own_columns = (jnp.arange(shards) == link.index)[:, None] * b_ada.astype(F32)[None, :]
    part = part + own_columns.reshape(-1)
    part = part.reshape(1, fsdp, latents * 6 * width)
    part = jnp.broadcast_to(part, (seq, fsdp, latents * 6 * width)).reshape(shards, -1)
    part = lax.all_to_all(part, AXES, 0, 0, tiled=True)
    modulation = jnp.sum(part, axis=0).reshape(latents, 1, 6 * width)
    modulation = cores(modulation)
    parts = [modulation[..., at * width : (at + 1) * width] for at in range(6)]
    shift_attn, scale_attn, gate_attn, shift_mlp, scale_mlp, gate_mlp = parts

    team_qkv = w_qkv.reshape(rows, 3, team, group).transpose(2, 0, 1, 3)
    team_qkv = link.exchange(team_qkv.reshape(team, rows, 3 * group), team_bits)
    half_tokens = halves(after(tokens, team_qkv))
    all_tokens = cores(half_tokens).astype(F32)
    my_qkv, begun = gather_rest(team_qkv.reshape(seq, 2 * rows, 3 * group))
    my_qkv = my_qkv.reshape(width, 3 * group)
    fc2_proj = jnp.concatenate([w_fc2, w_proj], axis=0)[None]
    fc2_proj, begun = gather_rest(fc2_proj, (begun,))
    my_fc2 = fc2_proj[0, :, :hidden_rows].reshape(hidden, width)
    full_proj = fc2_proj[0, :, hidden_rows:]
    full_proj = link.gather(full_proj, seq_bits, 0)
    full_proj = link.gather(full_proj, core_bit, 2).reshape(team, group, width)
    team_fc1 = w_fc1.reshape(rows, seq, rest, 2, hidden_rows).transpose(1, 3, 0, 2, 4)
    team_fc1 = after(team_fc1.reshape(team, rows, hidden), team_qkv)
    team_fc1 = link.exchange(team_fc1, team_bits)
    my_fc1, begun = gather_rest(team_fc1.reshape(seq, 2 * rows, hidden), (begun,))
    my_fc1 = my_fc1.reshape(width, hidden)
    all_cotangent = cores(halves(after(cotangent, half_tokens))).astype(F32)

    def own(value):
        return value[:latents]

    def own_rows(value):
        return lax.dynamic_slice_in_dim(value, half * local_len, local_len, 1)

    def team_part(left, right):
        other = dot_rt(left[own_flat:], right).astype(BF16)
        other = link.send(other, core_bit)
        total = dot_rt(left[:own_flat], right) + other.astype(F32)
        return total.reshape(latents, seq_len, width)

    def flat(value):
        return value.reshape(count * seq_len, -1)

    h_attn = flat(modulate(all_tokens, shift_attn, scale_attn).astype(BF16))
    bias_q = lax.dynamic_slice_in_dim(full_query, me * group, group, 0)
    bias_v = lax.dynamic_slice_in_dim(full_value, me * group, group, 0)
    bias_qkv = jnp.concatenate([bias_q, jnp.zeros_like(bias_q), bias_v]).astype(F32)
    qkv = (dot(h_attn, my_qkv) + bias_qkv).astype(BF16)
    qkv = qkv.reshape(count, seq_len, 3, heads, HD)
    query, key, value = qkv[:, :, 0], qkv[:, :, 1], qkv[:, :, 2]
    scores = jnp.einsum("lqhd,lkhd->lhqk", query, key, preferred_element_type=F32) * HD ** (-0.5)
    top = jnp.max(scores, axis=-1, keepdims=True)
    log_total = top + jnp.log(jnp.sum(jnp.exp(scores - top), axis=-1, keepdims=True))
    probs = jnp.exp(scores - log_total)
    probs_low = probs.astype(BF16)
    attended = jnp.einsum("lhqk,lkhd->lqhd", probs_low, value, preferred_element_type=F32)
    attended = attended.astype(BF16).reshape(count * seq_len, group)
    near = link.send(attended, core_bit)
    far = link.send(attended, seq_bits)
    across = link.send(far, core_bit)
    attn = bias_proj
    for step, piece in ((0, attended), (1, near), (2, far), (3, across)):
        if step % 2:
            piece = jnp.concatenate([piece[own_flat:], piece[:own_flat]], axis=0)
        attn = attn + dot(piece, link.pick(full_proj, me ^ step))
    attn = attn.reshape(count, seq_len, width)
    mid = all_tokens + gate_attn * attn

    h_mlp = flat(modulate(mid, shift_mlp, scale_mlp).astype(BF16))
    up = dot(h_mlp, my_fc1) + bias_fc1
    activated, gelu_back = jax.vjp(gelu_tanh, up)
    activated = activated.astype(BF16)
    grad_branch = flat((gate_mlp * all_cotangent).astype(BF16))
    grad_up = gelu_back(dot_rt(grad_branch, my_fc2))[0].astype(BF16)
    grad_h_mlp = team_part(grad_up, my_fc1).astype(BF16)
    sent_h_mlp = grad_h_mlp
    grad_h_mlp = grad_h_mlp.astype(F32) + link.send(grad_h_mlp, seq_bits).astype(F32)

    own_tokens = own(all_tokens)
    own_cotangent = own(all_cotangent)
    own_mid = own(mid)
    mlp_back = jax.vjp(modulate, own_mid, own(shift_mlp), own(scale_mlp))[1]
    grad_mid, grad_shift_mlp, grad_scale_mlp = mlp_back(grad_h_mlp)
    grad_mid = grad_mid + own_cotangent
    grad_gate_attn = jnp.sum(grad_mid * own(attn), axis=1, keepdims=True)
    own_grad_attn = (own(gate_attn) * grad_mid).astype(BF16)
    grad_attn = flat(cores(own_grad_attn))

    my_proj = link.pick(full_proj, me)
    grad_heads = dot_rt(grad_attn, my_proj).astype(BF16).reshape(count, seq_len, heads, HD)
    grad_probs = jnp.einsum("lqhd,lkhd->lhqk", grad_heads, value, preferred_element_type=F32)
    row_sums = jnp.sum(grad_probs * probs, axis=-1, keepdims=True)
    grad_scores = (probs * (grad_probs - row_sums)).astype(BF16)
    grad_value = jnp.einsum(
        "lhqk,lqhd->lkhd", probs_low, grad_heads, preferred_element_type=F32
    ).astype(BF16)
    grad_query = (
        jnp.einsum("lhqk,lkhd->lqhd", grad_scores, key, preferred_element_type=F32) * HD ** (-0.5)
    ).astype(BF16)
    grad_key = (
        jnp.einsum("lhqk,lqhd->lkhd", grad_scores, query, preferred_element_type=F32)
        * HD ** (-0.5)
    ).astype(BF16)
    grad_qkv = jnp.stack([grad_query, grad_key, grad_value], axis=2)
    grad_qkv = grad_qkv.reshape(count * seq_len, 3 * group)
    grad_h_attn = dot_rt(grad_qkv, my_qkv).reshape(count, seq_len, width)

    late = jnp.concatenate(
        [
            jnp.sum(grad_h_attn, axis=1),
            jnp.sum(grad_h_attn * normalize(all_tokens), axis=1),
        ],
        axis=-1,
    )
    late = late[:latents] + link.send(late[latents:], core_bit)
    late = late + link.send(late, seq_bits)
    late = all_rest(late.astype(BF16))

    activated, h_mlp = after((activated, h_mlp), sent_h_mlp)
    grad_fc2 = dot_lt(activated, grad_branch).astype(BF16)
    grad_fc2 = scatter_rest(
        grad_fc2.reshape(1, rest, hidden_rows, width), ((own_grad_attn,), (grad_qkv,))
    )[0]
    grad_fc1 = dot_lt(h_mlp, grad_up).astype(BF16)
    grad_fc1 = scatter_rest(
        grad_fc1.reshape(seq, rest, 2 * rows, hidden), ((own_grad_attn,), (grad_qkv,))
    ).astype(BF16)
    grad_fc1 = link.exchange(grad_fc1.reshape(team, rows, hidden), team_bits)
    grad_fc1 = grad_fc1.reshape(seq, 2, rows, rest, hidden_rows).transpose(2, 0, 3, 1, 4)
    grad_fc1 = grad_fc1.reshape(rows, -1).astype(F32)

    branch = dot(activated, my_fc2).reshape(2, latents, seq_len, width)
    branch = branch[0] + link.send(branch[1].astype(BF16), core_bit).astype(F32)
    branch = branch.reshape(latents, seq, local_len, width)
    branch = link.scatter(branch, seq_bits, 1, (own_grad_attn,)) + bias_fc2
    output = (own_rows(own_mid) + own(gate_mlp) * branch).astype(BF16)
    grad_gate_mlp = jnp.sum(cotangent.astype(F32) * branch, axis=1, keepdims=True)
    grad_gate_mlp = grad_gate_mlp + link.send(grad_gate_mlp, seq_bits)

    grad_w_qkv = dot_lt(h_attn, grad_qkv).astype(BF16)
    grad_w_qkv = scatter_rest(grad_w_qkv.reshape(seq, rest, 2 * rows, 3 * group)).astype(BF16)
    grad_w_qkv = link.exchange(grad_w_qkv.reshape(team, rows, 3 * group), team_bits)
    grad_w_qkv = grad_w_qkv.reshape(team, rows, 3, group).transpose(1, 2, 0, 3)
    grad_w_qkv = grad_w_qkv.reshape(rows, -1).astype(F32)
    grad_proj = dot_lt(attended, grad_attn).astype(BF16)
    grad_proj = grad_proj.reshape(rest // 2, 2, rows, width).swapaxes(0, 1)
    grad_proj = link.exchange(grad_proj, core_bit).reshape(1, rest, rows, width)
    grad_proj = scatter_rest(grad_proj)[0]

    other = link.send(grad_h_attn[latents:].astype(BF16), core_bit)
    grad_h_attn = grad_h_attn[:latents] + other.astype(F32)
    grad_h_attn = grad_h_attn.reshape(latents, seq, local_len, width)
    grad_h_attn = link.scatter(grad_h_attn, seq_bits, 1)
    attn_back = jax.vjp(
        modulate, tokens.astype(F32), own(shift_attn), own(scale_attn)
    )[1]
    grad_tokens = (own_rows(grad_mid) + attn_back(grad_h_attn)[0]).astype(BF16)

    early = jnp.concatenate(
        [grad_gate_attn, grad_shift_mlp, grad_scale_mlp, grad_gate_mlp], axis=-1
    )
    early = all_rest(early.reshape(latents, 4 * width).astype(BF16))
    grad_silu = dot_rt(early, w_ada[:, 2 * width :])
    grad_silu = grad_silu + dot_rt(late, w_ada[:, : 2 * width])
    grad_silu = grad_silu.reshape(1, fsdp, latents * rows)
    grad_silu = jnp.broadcast_to(grad_silu, (seq, fsdp, latents * rows)).reshape(shards, -1)
    grad_mod = jnp.concatenate([late, early], axis=1)
    grad_ada = dot_lt(all_cond, grad_mod)
    own_ada = b_ada.shape[0]
    grad_b_ada = lax.dynamic_slice_in_dim(grad_mod, link.index * own_ada, own_ada, 1)
    grad_b_ada = jnp.sum(grad_b_ada.astype(F32), axis=0)

    def column_sums(value):
        return jnp.sum(value.astype(F32), axis=0)

    everyone = 1.0 / team
    by_owner = [
        (column_sums(grad_branch) * everyone).reshape(shards, rows),
        (column_sums(grad_attn) * everyone).reshape(shards, rows),
    ]
    sums_qkv = column_sums(grad_qkv)
    in_team = (jnp.arange(team) == me)[:, None]
    for sums in (sums_qkv[:group], sums_qkv[2 * group :]):
        by_owner.append(jnp.where(in_team, sums[None, :], 0.0).reshape(shards, rows))
    sums_up = column_sums(grad_up).reshape(1, rest, 1, hidden_rows)
    in_seq = jnp.arange(seq).reshape(seq, 1, 1, 1) == half
    in_core = jnp.arange(2).reshape(1, 1, 2, 1) == core
    by_owner.append(jnp.where(in_seq & in_core, sums_up, 0.0).reshape(shards, hidden_rows))
    tail = jnp.concatenate([grad_silu] + by_owner, axis=1)
    tail = lax.all_to_all(tail, AXES, 0, 0, tiled=True)
    grad_silu = tail[:, :mine].reshape(shards, latents, rows).swapaxes(0, 1)
    grad_silu = grad_silu.reshape(latents, width)
    silu_back = jax.vjp(jax.nn.silu, cond_float)[1]
    grad_cond = silu_back(grad_silu)[0].astype(BF16)
    sums = jnp.sum(tail[:, mine:], axis=0)
    return (
        output,
        grad_tokens,
        grad_cond,
        grad_ada,
        grad_b_ada,
        grad_w_qkv,
        sums[2 * rows : 3 * rows],
        sums[3 * rows : 4 * rows],
        grad_proj,
        sums[rows : 2 * rows],
        grad_fc1,
        sums[4 * rows :],
        grad_fc2,
        sums[:rows],
    )


def solution(mesh):
    seq, fsdp = mesh.shape["seq"], mesh.shape["fsdp"]
    act = P("fsdp", "seq", None)
    matrix = P(AXES, None)
    vector = P(AXES)
    cond = P("fsdp", None)
    in_specs = (
        act, cond, matrix, vector, matrix, vector, vector, matrix, vector, matrix, vector, matrix,
        vector, act,
    )
    out_specs = (
        act, act, cond, matrix, vector, matrix, vector, vector, matrix, vector, matrix, vector,
        matrix, vector,
    )

    def layer(*args):
        return local(seq * fsdp, (seq, fsdp), *args)

    return jax.shard_map(layer, mesh=mesh, in_specs=in_specs, out_specs=out_specs, check_vma=False)
```

```python
import math

import jax
import jax.numpy as jnp
from jax import lax
from jax.experimental import pallas as pl
from jax.experimental.pallas import tpu as pltpu
from jax.sharding import PartitionSpec as P

HD = 64
AXES = ("seq", "fsdp")
F32 = jnp.float32
BF16 = jnp.bfloat16
VMEM_SPEC = pl.BlockSpec(memory_space=pltpu.VMEM)
SMEM_SPEC = pl.BlockSpec(memory_space=pltpu.SMEM)


def contract(left, right, left_dim, right_dim):
    return lax.dot_general(
        left, right, (((left_dim,), (right_dim,)), ((), ())), preferred_element_type=F32
    )


def dot(left, right):
    return contract(left, right, 1, 0)


def dot_rt(left, right):
    return contract(left, right, 1, 1)


def dot_lt(left, right):
    return contract(left, right, 0, 0)


def norm_parts(value):
    centre = value - jnp.mean(value, axis=-1, keepdims=True)
    variance = jnp.mean(centre * centre, axis=-1, keepdims=True)
    scale = lax.rsqrt(variance + 1e-06)
    return centre * scale, scale


def norm_back(norm, rate, grad):
    inner = jnp.mean(grad * norm, axis=-1, keepdims=True)
    return rate * (grad - jnp.mean(grad, axis=-1, keepdims=True) - norm * inner)


def after(value, *earlier):
    return lax.optimization_barrier((value,) + earlier)[0]


class Links:
    def __init__(self, devices):
        self.devices = devices
        self.index = lax.axis_index(AXES)

    def place(self, bits):
        spot = jnp.int32(0)
        for bit in bits:
            spot = spot * 2 + ((self.index >> bit) & 1)
        return spot

    def mask(self, bits, step):
        total = 0
        for at, bit in enumerate(reversed(bits)):
            total |= ((step >> at) & 1) << bit
        return total

    def groups(self, bits):
        steps = [self.mask(bits, step) for step in range(1 << len(bits))]
        return [
            [base | step for step in steps] for base in range(self.devices) if not base & steps[-1]
        ]

    def send(self, value, bits, step=1):
        mask = self.mask(bits, step)
        return lax.ppermute(value, AXES, [(i, i ^ mask) for i in range(self.devices)])

    def all_to_all(self, value, bits):
        return lax.all_to_all(
            value, AXES, 0, 0, tiled=True, axis_index_groups=self.groups(bits)
        )

    def flip(self, value, bits):
        shape = value.shape
        value = value.reshape((2,) * len(bits) + shape[1:])
        for axis, bit in enumerate(bits):
            first, second = jnp.split(value, 2, axis)
            turned = jnp.concatenate([second, first], axis)
            value = jnp.where(self.place([bit]) == 0, value, turned)
        return value.reshape(shape)

    def gather_step(self, value, bit, earlier=()):
        part = self.send(value, [bit])
        if earlier:
            value = after(value, *earlier)
        return jnp.concatenate([value, part], 0)

    def exchange(self, value, bits):
        value = self.flip(value, bits)
        parts = [value[:1]]
        for step in range(1, 1 << len(bits)):
            parts.append(self.send(value[step : step + 1], bits, step))
        return self.flip(jnp.concatenate(parts, 0), bits)

    def exchange_pieces(self, value, bits):
        spot = self.place(bits)
        parts = [self.pick(value, spot)]
        for step in range(1, 1 << len(bits)):
            parts.append(self.send(self.pick(value, spot ^ step), bits, step))
        return parts

    def gather(self, value, bits, axis):
        spot = self.place(bits)
        part = self.send(value, bits)
        shape = value.shape[:axis] + (2,) + value.shape[axis:]
        out = jnp.zeros(shape, value.dtype)
        out = lax.dynamic_update_index_in_dim(out, value, spot, axis)
        return lax.dynamic_update_index_in_dim(out, part, 1 - spot, axis)

    def pick(self, value, spot, axis=0):
        return lax.dynamic_index_in_dim(value, spot, axis, keepdims=False)

    def scatter(self, value, bits, earlier=()):
        spot = self.place(bits)
        arrived = []
        for step in range(1, 1 << len(bits)):
            arrived.append(self.send(self.pick(value, spot ^ step).astype(BF16), bits, step))
        total = self.pick(value, spot)
        if earlier:
            total = after(total, *earlier)
        total = total.astype(F32)
        for part in arrived:
            total = total + part.astype(F32)
        return total


def call(kernel, outs, *args, scalars=0, scratch=(), us=5):
    arrays = [jnp.reshape(arg, 1) for arg in args[:scalars]] + list(args[scalars:])
    return pl.pallas_call(
        kernel,
        out_shape=[jax.ShapeDtypeStruct(shape, dtype) for shape, dtype in outs],
        in_specs=[SMEM_SPEC] * scalars + [VMEM_SPEC] * (len(args) - scalars),
        out_specs=[VMEM_SPEC] * len(outs),
        scratch_shapes=[pltpu.VMEM(shape, dtype) for shape, dtype in scratch],
        compiler_params=pltpu.CompilerParams(vmem_limit_bytes=48 * 2**20),
        cost_estimate=pl.CostEstimate(
            flops=us * 10**9, bytes_accessed=us * 3 * 10**6, transcendentals=0
        ),
    )(*arrays)


def step_order(count):
    order = [0]
    while count > 1:
        count //= 2
        order = order + [at ^ count for at in order]
    return order


def interleave(own_ref, other_ref, out_ref, pair, high, swap=False):
    outer, inner, rows, cols = own_ref.shape
    for first, away in enumerate(step_order(outer)):
        to = jnp.bitwise_xor(high, away)
        for second in range(inner):
            out_ref[second, to, pair] = own_ref[first, second]
            piece = other_ref[first, second]
            if swap:
                piece = jnp.concatenate([piece[:, cols // 2 :], piece[:, : cols // 2]], axis=1)
            out_ref[second, to, 1 - pair] = piece


def interleave_call(own, other, pair, high):
    outer, inner, rows, cols = own.shape

    def kernel(pair_ref, high_ref, own_ref, other_ref, out_ref):
        interleave(own_ref, other_ref, out_ref, pair_ref[0], high_ref[0])

    shape = (inner, outer, 2, rows, cols)
    return call(kernel, [(shape, own.dtype)], pair, high, own, other, scalars=2, us=2)[0]


def attend(core, pair, high, mine, there, own_x, other_x, own_w, other_w, bias):
    latents, seq_len, width = own_x.shape[1:]
    count = 2 * latents
    columns = own_w.shape[3]
    group = columns // 3
    total = count * seq_len

    def kernel(
        core_ref, pair_ref, high_ref, mine_ref, there_ref, own_ref, other_ref, own_w_ref,
        other_w_ref, b_ref, mod_ref, h_ref, qkv_ref, out_ref, w_out_ref, w_ref,
    ):
        interleave(own_w_ref, other_w_ref, w_ref, pair_ref[0], high_ref[0])
        weight = w_ref[...].reshape(width, columns)
        w_out_ref[...] = weight
        core_at = core_ref[0]
        for side in range(2):
            row = jnp.bitwise_xor(core_at, side)
            for latent in range(latents):
                one, two = mine_ref[row, latent], there_ref[row, latent]
                first = jnp.where(core_at == 0, one, two)
                second = jnp.where(core_at == 0, two, one)
                mod_ref[side * latents + latent, 0:3] = first
                mod_ref[side * latents + latent, 3:6] = second
        for at in range(count):
            where = slice(at * seq_len, (at + 1) * seq_len)
            x = own_ref[0, at] if at < latents else other_ref[0, at - latents]
            norm = norm_parts(x.astype(F32))[0]
            shift, scale = mod_ref[at, 0:1], mod_ref[at, 1:2]
            h_low = (norm * (1.0 + scale) + shift).astype(BF16)
            h_ref[where] = h_low
            qkv = (dot(h_low, weight) + b_ref[...]).astype(BF16)
            qkv_ref[where] = qkv
            pieces = []
            for head in range(group // HD):
                query, key, value = (
                    qkv[:, part * group + head * HD : part * group + (head + 1) * HD]
                    for part in range(3)
                )
                probs = softmax(query, key).astype(BF16)
                pieces.append(dot(probs, value).astype(BF16))
            out_ref[where] = jnp.concatenate(pieces, axis=1)

    outs = [
        ((count, 6, width), F32),
        ((total, width), BF16),
        ((total, columns), BF16),
        ((total, group), BF16),
        ((width, columns), BF16),
    ]
    placed = (own_w.shape[1], own_w.shape[0], 2) + own_w.shape[2:]
    return call(
        kernel, outs, core, pair, high, mine, there, own_x, other_x, own_w, other_w, bias,
        scalars=3, scratch=[(placed, BF16)], us=6,
    )


def softmax(query, key):
    scores = dot_rt(query, key) * HD ** (-0.5)
    top = jnp.max(scores, axis=-1, keepdims=True)
    log_total = top + jnp.log(jnp.sum(jnp.exp(scores - top), axis=-1, keepdims=True))
    return jnp.exp(scores - log_total)


def feed(me, pair, high, pieces, proj, biases, own_x, other_x, mod, own_1, other_1, own_2, other_2):
    latents, seq_len, width = own_x.shape[1:]
    count = 2 * latents
    total = count * seq_len
    members = len(pieces)
    outer, seq, block, hidden = own_1.shape
    front = hidden // 2
    hidden_rows = hidden // (2 * outer)

    def kernel(me_ref, pair_ref, high_ref, *refs):
        piece_refs, refs = refs[:members], refs[members:]
        (
            proj_ref, bias_ref, own_ref, other_ref, mod_ref, own_1_ref, other_1_ref, own_2_ref,
            other_2_ref, attn_ref, mid_ref, h_own_ref, h_other_ref, keep_1_ref, send_1_ref,
            keep_2_ref, send_2_ref, out_own_ref, out_other_ref, gate_ref, sums_ref,
            fc1_ref, fc2_ref, h_ref, act_ref, up_ref, branch_ref, whole_ref,
        ) = refs
        interleave(own_1_ref, other_1_ref, fc1_ref, pair_ref[0], high_ref[0], swap=True)
        for at, away in enumerate(step_order(outer)):
            to = jnp.bitwise_xor(high_ref[0], away)
            fc2_ref[0, to] = own_2_ref[at, :hidden_rows]
            fc2_ref[1, to] = other_2_ref[at, :hidden_rows]
        fc1 = fc1_ref[...].reshape(width, hidden)
        fc2 = fc2_ref[...].reshape(hidden, width)
        sums_up, sums_branch = 0.0, 0.0
        for at in range(count):
            where = slice(at * seq_len, (at + 1) * seq_len)
            near = at % latents
            lane = slice(near * seq_len, (near + 1) * seq_len)
            away = (at + latents) % count
            away = slice(away * seq_len, (away + 1) * seq_len)
            x_ref = own_ref if at < latents else other_ref
            x, cotangent = x_ref[0, near].astype(F32), x_ref[1, near].astype(F32)
            mods = [mod_ref[at, part : part + 1] for part in range(6)]
            attn = bias_ref[0:1, :width]
            for step, piece_ref in enumerate(piece_refs):
                piece = piece_ref[away if step % 2 else where]
                attn = attn + dot(piece, proj_ref[jnp.bitwise_xor(me_ref[0], step)])
            mid = x + mods[2] * attn
            if at < latents:
                attn_ref[where] = attn
                mid_ref[where] = mid
            h_low = (norm_parts(mid)[0] * (1.0 + mods[4]) + mods[3]).astype(BF16)
            h_ref[where] = h_low
            up = dot(h_low, fc1) + bias_ref[1:2, :hidden]
            square = up * up
            bend = jnp.tanh(0.7978845608028654 * up * (1.0 + 0.044715 * square))
            act = (0.5 * up * (1.0 + bend)).astype(BF16)
            act_ref[where] = act
            slope = 0.7978845608028654 * (1.0 + 0.134145 * square)
            slope = 0.5 * (1.0 + bend) + 0.5 * up * (1.0 - bend * bend) * slope
            grad_branch = (mods[5] * cotangent).astype(BF16)
            branch_ref[where] = grad_branch
            grad_up = (slope * dot_rt(grad_branch, fc2)).astype(BF16)
            up_ref[where] = grad_up
            grad_h = dot_rt(grad_up, fc1)
            out = dot(act, fc2) + bias_ref[2:3, :width]
            gate_ref[at] = jnp.sum(cotangent * out, axis=0, keepdims=True)
            if at < latents:
                h_own_ref[lane] = grad_h
                out_own_ref[lane] = out
            else:
                h_other_ref[lane] = grad_h.astype(BF16)
                out_other_ref[lane] = out.astype(BF16)
            sums_branch = sums_branch + jnp.sum(
                grad_branch.astype(F32), axis=0, keepdims=True
            )
            sums_up = sums_up + jnp.sum(grad_up.astype(F32), axis=0, keepdims=True)
        sums_ref[0:1, :width] = sums_branch
        sums_ref[1:2, :hidden] = sums_up
        grad_2 = dot_lt(act_ref[...], branch_ref[...]).astype(BF16)
        keep_2_ref[...] = grad_2[:front]
        send_2_ref[...] = grad_2[front:]
        whole_ref[...] = dot_lt(h_ref[...], up_ref[...]).astype(BF16).reshape(whole_ref.shape)
        for first in range(seq):
            for second in range(outer):
                lane = slice(first * block, (first + 1) * block)
                at = first * outer + second
                keep_1_ref[second, lane] = whole_ref[at, pair_ref[0]]
                piece = whole_ref[at, 1 - pair_ref[0]]
                send_1_ref[second, lane] = jnp.concatenate(
                    [piece[:, front:], piece[:, :front]], axis=1
                )

    own_total = latents * seq_len
    wide = max(width, hidden)
    outs = [
        ((own_total, width), F32),
        ((own_total, width), F32),
        ((own_total, width), F32),
        ((own_total, width), BF16),
        ((outer, seq * block, hidden), BF16),
        ((outer, seq * block, hidden), BF16),
        ((front, width), BF16),
        ((front, width), BF16),
        ((own_total, width), F32),
        ((own_total, width), BF16),
        ((count, 1, width), F32),
        ((2, wide), F32),
    ]
    scratch = [
        ((seq, outer, 2, block, hidden), BF16),
        ((2, outer, hidden_rows, width), BF16),
        ((total, width), BF16),
        ((total, hidden), BF16),
        ((total, hidden), BF16),
        ((total, width), BF16),
        ((seq * outer, 2, block, hidden), BF16),
    ]
    args = pieces + [proj, biases, own_x, other_x, mod, own_1, other_1, own_2, other_2]
    return call(kernel, outs, me, pair, high, *args, scalars=3, scratch=scratch, us=12)


def norm_backward(mine, there, mid, attn, own_x, mod):
    latents, seq_len, width = own_x.shape[1:]

    def kernel(
        mine_ref, there_ref, mid_ref, attn_ref, x_ref, mod_ref, grad_ref, low_ref, sums_ref
    ):
        for at in range(latents):
            where = slice(at * seq_len, (at + 1) * seq_len)
            grad_h = mine_ref[where].astype(F32) + there_ref[where].astype(F32)
            norm, rate = norm_parts(mid_ref[where])
            grad = x_ref[1, at].astype(F32) + norm_back(
                norm, rate, grad_h * (1.0 + mod_ref[at, 4:5])
            )
            grad_ref[where] = grad
            low_ref[where] = (mod_ref[at, 2:3] * grad).astype(BF16)
            sums_ref[at, 0:1] = jnp.sum(grad * attn_ref[where], axis=0, keepdims=True)
            sums_ref[at, 1:2] = jnp.sum(grad_h, axis=0, keepdims=True)
            sums_ref[at, 2:3] = jnp.sum(grad_h * norm, axis=0, keepdims=True)

    outs = [
        ((latents * seq_len, width), F32),
        ((latents * seq_len, width), BF16),
        ((latents, 3, width), F32),
    ]
    return call(kernel, outs, mine, there, mid, attn, own_x, mod, us=3)


def attend_back(
    me, core, pair, own_grad, other_grad, proj, qkv, attended, near, h_low, weight, own_x, other_x,
    blocks,
):
    latents, seq_len, width = own_x.shape[1:]
    count = 2 * latents
    total, columns = qkv.shape
    group = columns // 3
    seq, high, block = blocks
    rows = block // 2
    third = rows // 3
    size = seq * block
    scale = HD ** (-0.5)

    def kernel(
        me_ref, core_ref, pair_ref, own_ref, other_ref, proj_ref, qkv_ref, att_ref, near_ref,
        h_ref, w_ref, own_x_ref, other_x_ref, keep_ref, send_ref, h_own_ref, h_other_ref,
        sums_ref, cols_ref, grads_ref, whole_ref, rows_ref,
    ):
        proj_rows = proj_ref[me_ref[0]]
        grad_mine, grad_near = 0.0, 0.0
        for at in range(count):
            where = slice(at * seq_len, (at + 1) * seq_len)
            away = (at + latents) % count
            away = slice(away * seq_len, (away + 1) * seq_len)
            lane = at % latents
            x = own_x_ref[0, lane] if at < latents else other_x_ref[0, lane]
            lane = slice(lane * seq_len, (lane + 1) * seq_len)
            grad_attn = own_ref[lane] if at < latents else other_ref[lane]
            grad_mine = grad_mine + dot_lt(att_ref[where], grad_attn)
            grad_near = grad_near + dot_lt(near_ref[away], grad_attn)
            grad_out = dot_rt(grad_attn, proj_rows).astype(BF16)
            pieces = [[], [], []]
            for head in range(group // HD):
                query, key, value = (
                    qkv_ref[where, part * group + head * HD : part * group + (head + 1) * HD]
                    for part in range(3)
                )
                grad_head = grad_out[:, head * HD : (head + 1) * HD]
                probs = softmax(query, key)
                grad_probs = dot_rt(grad_head, value)
                inner = jnp.sum(grad_probs * probs, axis=-1, keepdims=True)
                grad_scores = (probs * (grad_probs - inner)).astype(BF16)
                pieces[0].append((dot(grad_scores, key) * scale).astype(BF16))
                pieces[1].append((dot_lt(grad_scores, query) * scale).astype(BF16))
                pieces[2].append(dot_lt(probs.astype(BF16), grad_head).astype(BF16))
            grad_qkv = jnp.concatenate(sum(pieces, []), axis=1)
            grads_ref[where] = grad_qkv
            grad_h = dot_rt(grad_qkv, w_ref[...])
            norm = norm_parts(x.astype(F32))[0]
            sums_ref[at, 0:1] = jnp.sum(grad_h, axis=0, keepdims=True)
            sums_ref[at, 1:2] = jnp.sum(grad_h * norm, axis=0, keepdims=True)
            if at < latents:
                h_own_ref[lane] = grad_h
            else:
                h_other_ref[lane] = grad_h.astype(BF16)
        cols_ref[...] = jnp.sum(grads_ref[...].astype(F32), axis=0, keepdims=True)
        whole = dot_lt(h_ref[...], grads_ref[...]).astype(BF16)
        whole_ref[...] = whole.reshape(whole_ref.shape)
        half_rows = (high,) + rows_ref.shape[1:]
        rows_ref[pl.ds(core_ref[0] * high, high)] = grad_mine.reshape(half_rows)
        rows_ref[pl.ds((1 - core_ref[0]) * high, high)] = grad_near.reshape(half_rows)
        for to, out_ref in ((pair_ref[0], keep_ref), (1 - pair_ref[0], send_ref)):
            for second in range(high):
                for first in range(seq):
                    lane = slice(first * block, (first + 1) * block)
                    out_ref[second, lane] = whole_ref[first * high + second, to]
                piece = rows_ref[second * 2 + to, core_ref[0]].astype(BF16)
                out_ref[second, size : size + rows] = piece[:, :columns]
                out_ref[second, size + rows :] = jnp.concatenate(
                    [piece[at * third : (at + 1) * third, columns:] for at in range(3)], axis=1
                )

    own_total = latents * seq_len
    outs = [
        ((high, size + rows + third, columns), BF16),
        ((high, size + rows + third, columns), BF16),
        ((own_total, width), F32),
        ((own_total, width), BF16),
        ((count, 2, width), F32),
        ((1, columns), F32),
    ]
    scratch = [
        ((total, columns), BF16),
        ((seq * high, 2, block, columns), BF16),
        ((2 * high, 2, rows, width), F32),
    ]
    return call(
        kernel, outs, me, core, pair, own_grad, other_grad, proj, qkv, attended, near, h_low,
        weight, own_x, other_x, scalars=3, scratch=scratch, us=12,
    )


def join_fc1(me, pair, pieces, high):
    rows, hidden = pieces[0].shape
    wide = hidden // (2 * high)
    team = len(pieces)

    def kernel(me_ref, pair_ref, *refs):
        ins, out_ref, held_ref = refs[:team], refs[team], refs[team + 1]
        for step, piece_ref in enumerate(ins):
            piece = piece_ref[...].astype(F32)
            turned = jnp.concatenate([piece[:, hidden // 2 :], piece[:, : hidden // 2]], axis=1)
            held_ref[jnp.bitwise_xor(me_ref[0], step)] = jnp.where(
                pair_ref[0] == 0, piece, turned
            )
        out = []
        for first in range(team // 2):
            for second in range(high):
                for side in range(2):
                    at = (side * high + second) * wide
                    for core in range(2):
                        out.append(held_ref[first * 2 + core][:, at : at + wide])
        out_ref[...] = jnp.concatenate(out, axis=1)

    outs = [((rows, team * hidden), F32)]
    return call(
        kernel, outs, me, pair, *pieces, scalars=2, scratch=[((team, rows, hidden), F32)], us=2
    )[0]


def join_qkv(me, pieces):
    rows, columns = pieces[0].shape
    group = columns // 3
    team = len(pieces)

    def kernel(me_ref, *refs):
        ins, out_ref, held_ref = refs[:team], refs[team], refs[team + 1]
        for step, piece_ref in enumerate(ins):
            held_ref[jnp.bitwise_xor(me_ref[0], step)] = piece_ref[...].astype(F32)
        out = [
            held_ref[member][:, part * group : (part + 1) * group]
            for part in range(3)
            for member in range(team)
        ]
        out_ref[...] = jnp.concatenate(out, axis=1)

    outs = [((rows, team * columns), F32)]
    return call(
        kernel, outs, me, *pieces, scalars=1, scratch=[((team, rows, columns), F32)], us=2
    )[0]


def local(
    shards,
    split,
    tokens,
    cond,
    w_ada,
    b_ada,
    w_qkv,
    b_query,
    b_value,
    w_proj,
    b_proj,
    w_fc1,
    b_fc1,
    w_fc2,
    b_fc2,
    cotangent,
):
    seq, fsdp = split
    link = Links(shards)
    low_bits = int(math.log2(fsdp))
    core_bit = [0]
    seq_bits = list(range(low_bits, int(math.log2(shards))))[::-1]
    pair_bit, high_bits = [1], list(range(2, low_bits))[::-1]
    team_bits = seq_bits + core_bit
    team = seq * 2
    rest = fsdp // 2
    high = rest // 2
    core, half, me = link.place(core_bit), link.place(seq_bits), link.place(team_bits)
    pair, spot = link.place(pair_bit), link.place(high_bits)
    latents, local_len, width = tokens.shape
    seq_len = seq * local_len
    rows = w_qkv.shape[0]
    hidden_rows = w_fc2.shape[0]
    hidden = hidden_rows * rest
    group = width // team
    columns = 3 * group
    count = 2 * latents
    chips = shards // 2

    direct = [jnp.concatenate([w_fc2, w_proj], axis=0)[None]]
    for bit in high_bits:
        direct.append(link.gather_step(direct[-1], bit))

    cond_float = cond.astype(F32)
    silu_cond = jax.nn.silu(cond_float).astype(BF16)
    mine = latents * rows
    cond_blocks = silu_cond.reshape(latents, seq, fsdp, rows)
    cond_blocks = link.pick(cond_blocks, half, 1).swapaxes(0, 1).reshape(fsdp, mine)
    small = 4 * rows + hidden_rows
    bias_row = sum(
        jnp.pad(bias[None], ((0, 0), (start, mine + small - start - bias.shape[0])))
        for start, bias in (
            (mine, b_query), (mine + rows, b_value), (mine + 2 * rows, b_proj),
            (mine + 3 * rows, b_fc2), (mine + 4 * rows, b_fc1),
        )
    )
    to_all = jnp.pad(cond_blocks, ((0, 0), (0, small))) + bias_row
    from_all = lax.all_to_all(to_all, "fsdp", 0, 0, tiled=True)
    all_cond = from_all[:, :mine].reshape(fsdp * latents, rows)
    biases = from_all[:, mine:]
    bias_q, bias_v = (
        lax.dynamic_slice_in_dim(
            biases[:, at * rows : (at + 1) * rows].reshape(1, -1), core * group, group, 1
        ).astype(F32)
        for at in range(2)
    )
    bias_qkv = jnp.concatenate([bias_q, jnp.zeros_like(bias_q), bias_v], axis=1)
    bias_fc1 = biases[:, 4 * rows :].reshape(high, 2, 2, hidden_rows)
    bias_fc1 = link.flip(link.pick(bias_fc1, core, 2).swapaxes(0, 1), pair_bit)
    bias_fc1 = bias_fc1.reshape(1, hidden).astype(F32)

    acts = jnp.stack([tokens, cotangent]).reshape(-1, 1, local_len, width)
    acts = interleave_call(acts, link.send(acts, seq_bits), half, jnp.int32(0))
    acts = acts.reshape(2, latents, seq_len, width)
    team_qkv = w_qkv.reshape(rows, 3, team, group).transpose(2, 0, 1, 3)
    team_fc1 = w_fc1.reshape(rows, seq, high, 2, 2, hidden_rows).transpose(3, 2, 1, 4, 0, 5)
    team_fc1 = link.flip(team_fc1, pair_bit).transpose(2, 3, 4, 0, 1, 5)
    team_part = jnp.concatenate(
        [team_qkv.reshape(team, rows, columns), team_fc1.reshape(team, rows, hidden)], axis=2
    )
    team_part = link.exchange(after(team_part, from_all), team_bits)
    part = dot(all_cond, w_ada)
    own_columns = (jnp.arange(shards) == link.index)[:, None] * b_ada.astype(F32)[None, :]
    part = after(part + own_columns.reshape(-1), acts, team_part, direct[1])
    part = part.reshape(fsdp * latents, 2, 3 * width)
    part = link.pick(part, core, 1) + link.send(link.pick(part, 1 - core, 1), core_bit)
    part = part.reshape(1, rest, count * 3 * width)
    part = jnp.broadcast_to(part, (seq, rest, count * 3 * width)).reshape(chips, -1)
    sent_part = part
    part = link.all_to_all(part, seq_bits + [*high_bits, *pair_bit])

    team_qkv = team_part[:, :, :columns].reshape(1, seq, 2 * rows, columns)
    team_fc1 = team_part[:, :, columns:].reshape(1, seq, 2 * rows, hidden)
    direct_own = direct[-1]
    direct_other = link.send(direct_own, pair_bit)
    steps = [team_qkv]
    for bit in high_bits:
        ready = (direct_own,) if bit == high_bits[0] else (part,)
        steps.append(link.gather_step(steps[-1], bit, ready))
    qkv_own = steps[-1]
    qkv_other = link.send(qkv_own, pair_bit)
    other_acts = link.send(acts, core_bit)
    fc1_steps = [after(team_fc1, steps[1])]
    for bit in high_bits:
        fc1_steps.append(link.gather_step(fc1_steps[-1], bit, (qkv_own,)))
    fc1_own = fc1_steps[-1]
    fc1_other = link.send(fc1_own, pair_bit)
    part = after(part, fc1_steps[1], other_acts)
    modulation = jnp.sum(part, axis=0).reshape(2, latents, 3, width)
    full_proj = interleave_call(
        direct_own[:, None, hidden_rows:], direct_other[:, None, hidden_rows:], pair, spot
    )
    half_proj = full_proj
    full_proj = link.gather(full_proj.reshape(rest, rows, width), seq_bits, 0)
    full_proj = link.gather(full_proj, core_bit, 2).reshape(team, group, width)
    bias_out = link.gather(after(biases, sent_part)[:, 2 * rows : 4 * rows], seq_bits, 0)
    bias_proj, bias_fc2 = (
        bias_out[:, :, at * rows : (at + 1) * rows].reshape(1, width).astype(F32) for at in range(2)
    )
    wide = max(width, hidden)
    feed_biases = jnp.concatenate(
        [
            jnp.pad(bias, ((0, 0), (0, wide - bias.shape[1])))
            for bias in (bias_proj, bias_fc1, bias_fc2 * (1.0 / team))
        ],
        axis=0,
    )

    mod, h_attn, qkv, attended, my_qkv = attend(
        core, pair, spot, modulation, link.send(modulation, core_bit), acts, other_acts,
        after(qkv_own, half_proj, fc1_own),
        qkv_other, bias_qkv,
    )

    near = link.send(attended, core_bit)
    far = link.send(attended, seq_bits)
    across = link.send(far, core_bit)
    (
        attn, mid, grad_h, other_h, keep_fc1, send_fc1, keep_fc2, send_fc2, branch, other_branch,
        grad_gate_mlp, sums_mlp,
    ) = feed(
        me, pair, spot, [attended, near, far, across], full_proj, feed_biases, acts, other_acts,
        mod, fc1_own, fc1_other, direct_own, direct_other,
    )
    grad_h = (grad_h + link.send(other_h, core_bit).astype(F32)).astype(BF16)
    there_h = link.send(grad_h, seq_bits)
    sent_fc2 = link.send(send_fc2, pair_bit)
    sent_fc1 = link.send(send_fc1, pair_bit)
    sent_branch = link.send(other_branch, core_bit)
    grad_mid, grad_attn, sums_mid = norm_backward(grad_h, there_h, mid, attn, acts, mod)
    other_attn = link.send(grad_attn, core_bit)
    grad_fc2 = after(keep_fc2, grad_attn).astype(F32) + sent_fc2.astype(F32)
    grad_fc2 = grad_fc2.astype(BF16).reshape(high, hidden_rows, width)
    keep_qkv, send_qkv, grad_h_attn, other_h_attn, sums_attn, sums_qkv = attend_back(
        me, core, pair, after(grad_attn, grad_fc2), other_attn, full_proj, qkv, attended, near,
        h_attn, my_qkv, acts, other_acts, (seq, high, 2 * rows),
    )

    late = jnp.concatenate([sums_attn, grad_gate_mlp], axis=1)
    late = late[:latents] + link.send(late[latents:], core_bit)
    grad_fc2 = link.scatter(grad_fc2, high_bits)
    late = after(late, grad_fc2)
    late = late + link.send(late, seq_bits)
    grad_mod = jnp.concatenate([late[:, :2], sums_mid, late[:, 2:]], axis=1)
    grad_mod = grad_mod.reshape(1, -1, 128).astype(BF16)
    grad_mod = jnp.broadcast_to(grad_mod, (fsdp,) + grad_mod.shape[1:])
    sent_mod = grad_mod
    grad_mod = lax.all_to_all(grad_mod, "fsdp", 0, 0, tiled=True)
    grad_mod = grad_mod.reshape(fsdp * latents, 6 * width)

    sent_qkv = link.send(send_qkv, pair_bit)
    grad_silu = dot_rt(after(grad_mod, sent_qkv), w_ada).reshape(1, fsdp, mine)
    grad_silu = jnp.broadcast_to(grad_silu, (seq, fsdp, mine)).reshape(shards, -1)
    grad_ada = dot_lt(all_cond, grad_mod)
    own_ada = b_ada.shape[0]
    grad_b_ada = lax.dynamic_slice_in_dim(grad_mod, link.index * own_ada, own_ada, 1)
    grad_b_ada = jnp.sum(grad_b_ada.astype(F32), axis=0)
    everyone = 1.0 / team
    sums_proj = jnp.sum(grad_attn.astype(F32), axis=0) * (1.0 / seq)
    sums_branch, sums_up = sums_mlp[0, :width] * everyone, sums_mlp[1, :hidden]
    sums_proj, sums_branch, sums_up, sums_qkv = after(
        (sums_proj, sums_branch, sums_up, sums_qkv), sent_mod
    )
    in_team = (jnp.arange(team) == me)[:, None]
    by_owner = [sums_branch.reshape(shards, rows), sums_proj.reshape(shards, rows)]
    for sums in (sums_qkv[:, :group], sums_qkv[:, 2 * group :]):
        by_owner.append(jnp.where(in_team, sums, 0.0).reshape(shards, rows))
    sums_up = link.flip(sums_up.reshape(2, high, hidden_rows), pair_bit).swapaxes(0, 1)
    sums_up = sums_up.reshape(1, rest, 1, hidden_rows)
    in_seq = jnp.arange(seq).reshape(seq, 1, 1, 1) == half
    in_core = jnp.arange(2).reshape(1, 1, 2, 1) == core
    by_owner.append(jnp.where(in_seq & in_core, sums_up, 0.0).reshape(shards, hidden_rows))
    tail = jnp.concatenate([grad_silu] + by_owner, axis=1)
    sent_tail = tail
    tail = lax.all_to_all(tail, AXES, 0, 0, tiled=True)
    grad_fc1 = after(keep_fc1, late).astype(F32) + sent_fc1.astype(F32)
    grad_fc1 = link.scatter(grad_fc1.astype(BF16), high_bits, (sent_tail,)).astype(BF16)
    grad_fc1 = link.exchange_pieces(grad_fc1.reshape(team, rows, hidden), team_bits)
    grad_fc1 = join_fc1(me, pair, grad_fc1, high)
    grad_qkv = after(keep_qkv, sent_mod).astype(F32) + sent_qkv.astype(F32)
    grad_qkv = link.scatter(grad_qkv.astype(BF16), high_bits, (sent_tail,))
    size = team * rows
    grad_proj = grad_qkv[size : size + rows]
    last = grad_qkv[size + rows :].reshape(rows // 3, 3, group).swapaxes(0, 1)
    grad_proj = jnp.concatenate([grad_proj, last.reshape(rows, group)], axis=1)
    grad_qkv = grad_qkv[:size].astype(BF16).reshape(team, rows, columns)
    grad_qkv = join_qkv(me, link.exchange_pieces(grad_qkv, team_bits))

    def own_rows(value):
        value = value.reshape(latents, seq_len, -1)
        return lax.dynamic_slice_in_dim(value, half * local_len, local_len, 1)

    branch = after(branch, other_attn) + sent_branch.astype(F32)
    grad_h_attn = after(grad_h_attn, sent_mod) + link.send(other_h_attn, core_bit).astype(F32)
    both = jnp.stack([branch, grad_h_attn]).reshape(2, latents, seq, local_len, width)
    both = link.scatter(jnp.moveaxis(both, 2, 0), seq_bits, (sent_tail,))
    output = (own_rows(mid) + mod[:latents, 5:6] * both[0]).astype(BF16)
    norm, rate = norm_parts(tokens.astype(F32))
    grad_tokens = norm_back(norm, rate, both[1] * (1.0 + mod[:latents, 1:2]))
    grad_tokens = (own_rows(grad_mid) + grad_tokens).astype(BF16)

    grad_silu = tail[:, :mine].reshape(shards, latents, rows).swapaxes(0, 1)
    grad_silu = grad_silu.reshape(latents, width)
    silu_back = jax.vjp(jax.nn.silu, cond_float)[1]
    grad_cond = silu_back(grad_silu)[0].astype(BF16)
    sums = jnp.sum(tail[:, mine:], axis=0)
    return (
        output,
        grad_tokens,
        grad_cond,
        grad_ada,
        grad_b_ada,
        grad_qkv,
        sums[2 * rows : 3 * rows],
        sums[3 * rows : 4 * rows],
        grad_proj,
        sums[rows : 2 * rows],
        grad_fc1,
        sums[4 * rows :],
        grad_fc2,
        sums[:rows],
    )


def solution(mesh):
    seq, fsdp = mesh.shape["seq"], mesh.shape["fsdp"]
    act = P("fsdp", "seq", None)
    matrix = P(AXES, None)
    vector = P(AXES)
    cond = P("fsdp", None)
    in_specs = (
        act, cond, matrix, vector, matrix, vector, vector, matrix, vector, matrix, vector, matrix,
        vector, act,
    )
    out_specs = (
        act, act, cond, matrix, vector, matrix, vector, vector, matrix, vector, matrix, vector,
        matrix, vector,
    )

    def layer(*args):
        return local(seq * fsdp, (seq, fsdp), *args)

    return jax.shard_map(layer, mesh=mesh, in_specs=in_specs, out_specs=out_specs, check_vma=False)
```

```python
import math

import jax
import jax.numpy as jnp
from jax import lax
from jax.experimental import pallas as pl
from jax.experimental.pallas import tpu as pltpu
from jax.sharding import PartitionSpec as P

HD = 64
AXES = ("seq", "fsdp")
F32 = jnp.float32
BF16 = jnp.bfloat16
VMEM_SPEC = pl.BlockSpec(memory_space=pltpu.VMEM)
SMEM_SPEC = pl.BlockSpec(memory_space=pltpu.SMEM)


def contract(left, right, left_dim, right_dim):
    return lax.dot_general(
        left, right, (((left_dim,), (right_dim,)), ((), ())), preferred_element_type=F32
    )


def dot(left, right):
    return contract(left, right, 1, 0)


def dot_rt(left, right):
    return contract(left, right, 1, 1)


def dot_lt(left, right):
    return contract(left, right, 0, 0)


def norm_parts(value):
    centre = value - jnp.mean(value, axis=-1, keepdims=True)
    variance = jnp.mean(centre * centre, axis=-1, keepdims=True)
    scale = lax.rsqrt(variance + 1e-06)
    return centre * scale, scale


def norm_back(norm, rate, grad):
    inner = jnp.mean(grad * norm, axis=-1, keepdims=True)
    return rate * (grad - jnp.mean(grad, axis=-1, keepdims=True) - norm * inner)


def after(value, *earlier):
    return lax.optimization_barrier((value,) + earlier)[0]


class Links:
    def __init__(self, devices):
        self.devices = devices
        self.index = lax.axis_index(AXES)

    def place(self, bits):
        spot = jnp.int32(0)
        for bit in bits:
            spot = spot * 2 + ((self.index >> bit) & 1)
        return spot

    def mask(self, bits, step):
        total = 0
        for at, bit in enumerate(reversed(bits)):
            total |= ((step >> at) & 1) << bit
        return total

    def groups(self, bits):
        steps = [self.mask(bits, step) for step in range(1 << len(bits))]
        return [
            [base | step for step in steps] for base in range(self.devices) if not base & steps[-1]
        ]

    def send(self, value, bits, step=1):
        mask = self.mask(bits, step)
        return lax.ppermute(value, AXES, [(i, i ^ mask) for i in range(self.devices)])

    def all_to_all(self, value, bits):
        return lax.all_to_all(
            value, AXES, 0, 0, tiled=True, axis_index_groups=self.groups(bits)
        )

    def flip(self, value, bits):
        shape = value.shape
        value = value.reshape((2,) * len(bits) + shape[1:])
        for axis, bit in enumerate(bits):
            first, second = jnp.split(value, 2, axis)
            turned = jnp.concatenate([second, first], axis)
            value = jnp.where(self.place([bit]) == 0, value, turned)
        return value.reshape(shape)

    def gather_step(self, value, bit, earlier=()):
        part = self.send(value, [bit])
        if earlier:
            value = after(value, *earlier)
        return jnp.concatenate([value, part], 0)

    def exchange(self, value, bits):
        value = self.flip(value, bits)
        parts = [value[:1]]
        for step in range(1, 1 << len(bits)):
            parts.append(self.send(value[step : step + 1], bits, step))
        return self.flip(jnp.concatenate(parts, 0), bits)

    def exchange_pieces(self, value, bits):
        spot = self.place(bits)
        parts = [self.pick(value, spot)]
        for step in range(1, 1 << len(bits)):
            parts.append(self.send(self.pick(value, spot ^ step), bits, step))
        return parts

    def gather(self, value, bits, axis):
        spot = self.place(bits)
        part = self.send(value, bits)
        shape = value.shape[:axis] + (2,) + value.shape[axis:]
        out = jnp.zeros(shape, value.dtype)
        out = lax.dynamic_update_index_in_dim(out, value, spot, axis)
        return lax.dynamic_update_index_in_dim(out, part, 1 - spot, axis)

    def pick(self, value, spot, axis=0):
        return lax.dynamic_index_in_dim(value, spot, axis, keepdims=False)

    def scatter(self, value, bits, earlier=(), first=()):
        for bit in reversed(bits):
            spot = self.place([bit])
            value = value.reshape((-1, 2) + value.shape[1:])
            part = self.send(self.pick(value, 1 - spot, 1).astype(BF16), [bit])
            value = self.pick(value, spot, 1)
            ready = earlier if bit == bits[0] else first
            if ready:
                value = after(value, *ready)
            value = value.astype(F32) + part.astype(F32)
            if bit != bits[0]:
                value = value.astype(BF16)
        return value[0]


def call(kernel, outs, *args, scalars=0, scratch=(), us=5):
    arrays = [jnp.reshape(arg, 1) for arg in args[:scalars]] + list(args[scalars:])
    return pl.pallas_call(
        kernel,
        out_shape=[jax.ShapeDtypeStruct(shape, dtype) for shape, dtype in outs],
        in_specs=[SMEM_SPEC] * scalars + [VMEM_SPEC] * (len(args) - scalars),
        out_specs=[VMEM_SPEC] * len(outs),
        scratch_shapes=[pltpu.VMEM(shape, dtype) for shape, dtype in scratch],
        compiler_params=pltpu.CompilerParams(vmem_limit_bytes=48 * 2**20),
        cost_estimate=pl.CostEstimate(
            flops=us * 10**8, bytes_accessed=us * 3 * 10**5, transcendentals=0
        ),
    )(*arrays)


def step_order(count):
    order = [0]
    while count > 1:
        count //= 2
        order = order + [at ^ count for at in order]
    return order


def interleave(own_ref, other_ref, out_ref, pair, high, swap=False):
    outer, inner, rows, cols = own_ref.shape
    for first, away in enumerate(step_order(outer)):
        to = jnp.bitwise_xor(high, away)
        for second in range(inner):
            out_ref[second, to, pair] = own_ref[first, second]
            piece = other_ref[first, second]
            if swap:
                piece = jnp.concatenate([piece[:, cols // 2 :], piece[:, : cols // 2]], axis=1)
            out_ref[second, to, 1 - pair] = piece


def interleave_call(own, other, pair, high):
    outer, inner, rows, cols = own.shape

    def kernel(pair_ref, high_ref, own_ref, other_ref, out_ref):
        interleave(own_ref, other_ref, out_ref, pair_ref[0], high_ref[0])

    shape = (inner, outer, 2, rows, cols)
    return call(kernel, [(shape, own.dtype)], pair, high, own, other, scalars=2, us=2)[0]


def attend(core, pair, high, mine, there, own_x, other_x, own_w, other_w, bias):
    latents, seq_len, width = own_x.shape[1:]
    count = 2 * latents
    columns = own_w.shape[3]
    group = columns // 3
    total = count * seq_len

    def kernel(
        core_ref, pair_ref, high_ref, mine_ref, there_ref, own_ref, other_ref, own_w_ref,
        other_w_ref, b_ref, mod_ref, h_ref, qkv_ref, out_ref, w_out_ref, w_ref,
    ):
        interleave(own_w_ref, other_w_ref, w_ref, pair_ref[0], high_ref[0])
        weight = w_ref[...].reshape(width, columns)
        w_out_ref[...] = weight
        core_at = core_ref[0]
        for side in range(2):
            row = jnp.bitwise_xor(core_at, side)
            for latent in range(latents):
                one, two = mine_ref[row, latent], there_ref[row, latent]
                first = jnp.where(core_at == 0, one, two)
                second = jnp.where(core_at == 0, two, one)
                mod_ref[side * latents + latent, 0:3] = first
                mod_ref[side * latents + latent, 3:6] = second
        for at in range(count):
            where = slice(at * seq_len, (at + 1) * seq_len)
            x = own_ref[0, at] if at < latents else other_ref[0, at - latents]
            norm = norm_parts(x.astype(F32))[0]
            shift, scale = mod_ref[at, 0:1], mod_ref[at, 1:2]
            h_low = (norm * (1.0 + scale) + shift).astype(BF16)
            h_ref[where] = h_low
            qkv = (dot(h_low, weight) + b_ref[...]).astype(BF16)
            qkv_ref[where] = qkv
            pieces = []
            for head in range(group // HD):
                query, key, value = (
                    qkv[:, part * group + head * HD : part * group + (head + 1) * HD]
                    for part in range(3)
                )
                probs = softmax(query, key).astype(BF16)
                pieces.append(dot(probs, value).astype(BF16))
            out_ref[where] = jnp.concatenate(pieces, axis=1)

    outs = [
        ((count, 6, width), F32),
        ((total, width), BF16),
        ((total, columns), BF16),
        ((total, group), BF16),
        ((width, columns), BF16),
    ]
    placed = (own_w.shape[1], own_w.shape[0], 2) + own_w.shape[2:]
    return call(
        kernel, outs, core, pair, high, mine, there, own_x, other_x, own_w, other_w, bias,
        scalars=3, scratch=[(placed, BF16)], us=6,
    )


def softmax(query, key):
    scores = dot_rt(query, key) * HD ** (-0.5)
    top = jnp.max(scores, axis=-1, keepdims=True)
    log_total = top + jnp.log(jnp.sum(jnp.exp(scores - top), axis=-1, keepdims=True))
    return jnp.exp(scores - log_total)


def feed(me, pair, high, pieces, proj, biases, own_x, other_x, mod, own_1, other_1, own_2, other_2):
    latents, seq_len, width = own_x.shape[1:]
    count = 2 * latents
    total = count * seq_len
    members = len(pieces)
    outer, seq, block, hidden = own_1.shape
    front = hidden // 2
    hidden_rows = hidden // (2 * outer)

    def kernel(me_ref, pair_ref, high_ref, *refs):
        piece_refs, refs = refs[:members], refs[members:]
        (
            proj_ref, bias_ref, own_ref, other_ref, mod_ref, own_1_ref, other_1_ref, own_2_ref,
            other_2_ref, attn_ref, mid_ref, h_own_ref, h_other_ref, keep_1_ref, send_1_ref,
            keep_2_ref, send_2_ref, out_own_ref, out_other_ref, gate_ref, sums_ref,
            fc1_ref, fc2_ref, h_ref, act_ref, up_ref, branch_ref, whole_ref,
        ) = refs
        interleave(own_1_ref, other_1_ref, fc1_ref, pair_ref[0], high_ref[0], swap=True)
        for at, away in enumerate(step_order(outer)):
            to = jnp.bitwise_xor(high_ref[0], away)
            fc2_ref[0, to] = own_2_ref[at, :hidden_rows]
            fc2_ref[1, to] = other_2_ref[at, :hidden_rows]
        fc1 = fc1_ref[...].reshape(width, hidden)
        fc2 = fc2_ref[...].reshape(hidden, width)
        sums_up, sums_branch = 0.0, 0.0
        for at in range(count):
            where = slice(at * seq_len, (at + 1) * seq_len)
            near = at % latents
            lane = slice(near * seq_len, (near + 1) * seq_len)
            away = (at + latents) % count
            away = slice(away * seq_len, (away + 1) * seq_len)
            x_ref = own_ref if at < latents else other_ref
            x, cotangent = x_ref[0, near].astype(F32), x_ref[1, near].astype(F32)
            mods = [mod_ref[at, part : part + 1] for part in range(6)]
            attn = bias_ref[0:1, :width]
            for step, piece_ref in enumerate(piece_refs):
                piece = piece_ref[away if step % 2 else where]
                attn = attn + dot(piece, proj_ref[jnp.bitwise_xor(me_ref[0], step)])
            mid = x + mods[2] * attn
            if at < latents:
                attn_ref[where] = attn
                mid_ref[where] = mid
            h_low = (norm_parts(mid)[0] * (1.0 + mods[4]) + mods[3]).astype(BF16)
            h_ref[where] = h_low
            up = dot(h_low, fc1) + bias_ref[1:2, :hidden]
            square = up * up
            bend = jnp.tanh(0.7978845608028654 * up * (1.0 + 0.044715 * square))
            act = (0.5 * up * (1.0 + bend)).astype(BF16)
            act_ref[where] = act
            slope = 0.7978845608028654 * (1.0 + 0.134145 * square)
            slope = 0.5 * (1.0 + bend) + 0.5 * up * (1.0 - bend * bend) * slope
            grad_branch = (mods[5] * cotangent).astype(BF16)
            branch_ref[where] = grad_branch
            grad_up = (slope * dot_rt(grad_branch, fc2)).astype(BF16)
            up_ref[where] = grad_up
            grad_h = dot_rt(grad_up, fc1)
            out = dot(act, fc2) + bias_ref[2:3, :width]
            gate_ref[at] = jnp.sum(cotangent * out, axis=0, keepdims=True)
            if at < latents:
                h_own_ref[lane] = grad_h
                out_own_ref[lane] = out
            else:
                h_other_ref[lane] = grad_h.astype(BF16)
                out_other_ref[lane] = out.astype(BF16)
            sums_branch = sums_branch + jnp.sum(
                grad_branch.astype(F32), axis=0, keepdims=True
            )
            sums_up = sums_up + jnp.sum(grad_up.astype(F32), axis=0, keepdims=True)
        sums_ref[0:1, :width] = sums_branch
        sums_ref[1:2, :hidden] = sums_up
        grad_2 = dot_lt(act_ref[...], branch_ref[...]).astype(BF16)
        keep_2_ref[...] = grad_2[:front]
        send_2_ref[...] = grad_2[front:]
        whole_ref[...] = dot_lt(h_ref[...], up_ref[...]).astype(BF16).reshape(whole_ref.shape)
        for first in range(seq):
            for second in range(outer):
                lane = slice(first * block, (first + 1) * block)
                at = first * outer + second
                keep_1_ref[second, lane] = whole_ref[at, pair_ref[0]]
                piece = whole_ref[at, 1 - pair_ref[0]]
                send_1_ref[second, lane] = jnp.concatenate(
                    [piece[:, front:], piece[:, :front]], axis=1
                )

    own_total = latents * seq_len
    wide = max(width, hidden)
    outs = [
        ((own_total, width), F32),
        ((own_total, width), F32),
        ((own_total, width), F32),
        ((own_total, width), BF16),
        ((outer, seq * block, hidden), BF16),
        ((outer, seq * block, hidden), BF16),
        ((front, width), BF16),
        ((front, width), BF16),
        ((own_total, width), F32),
        ((own_total, width), BF16),
        ((count, 1, width), F32),
        ((2, wide), F32),
    ]
    scratch = [
        ((seq, outer, 2, block, hidden), BF16),
        ((2, outer, hidden_rows, width), BF16),
        ((total, width), BF16),
        ((total, hidden), BF16),
        ((total, hidden), BF16),
        ((total, width), BF16),
        ((seq * outer, 2, block, hidden), BF16),
    ]
    args = pieces + [proj, biases, own_x, other_x, mod, own_1, other_1, own_2, other_2]
    return call(kernel, outs, me, pair, high, *args, scalars=3, scratch=scratch, us=12)


def norm_backward(mine, there, mid, attn, own_x, mod):
    latents, seq_len, width = own_x.shape[1:]

    def kernel(
        mine_ref, there_ref, mid_ref, attn_ref, x_ref, mod_ref, grad_ref, low_ref, sums_ref
    ):
        for at in range(latents):
            where = slice(at * seq_len, (at + 1) * seq_len)
            grad_h = mine_ref[where].astype(F32) + there_ref[where].astype(F32)
            norm, rate = norm_parts(mid_ref[where])
            grad = x_ref[1, at].astype(F32) + norm_back(
                norm, rate, grad_h * (1.0 + mod_ref[at, 4:5])
            )
            grad_ref[where] = grad
            low_ref[where] = (mod_ref[at, 2:3] * grad).astype(BF16)
            sums_ref[at, 0:1] = jnp.sum(grad * attn_ref[where], axis=0, keepdims=True)
            sums_ref[at, 1:2] = jnp.sum(grad_h, axis=0, keepdims=True)
            sums_ref[at, 2:3] = jnp.sum(grad_h * norm, axis=0, keepdims=True)

    outs = [
        ((latents * seq_len, width), F32),
        ((latents * seq_len, width), BF16),
        ((latents, 3, width), F32),
    ]
    return call(kernel, outs, mine, there, mid, attn, own_x, mod, us=3)


def attend_back(
    me, core, pair, own_grad, other_grad, proj, qkv, attended, near, h_low, weight, own_x, other_x,
    blocks,
):
    latents, seq_len, width = own_x.shape[1:]
    count = 2 * latents
    total, columns = qkv.shape
    group = columns // 3
    seq, high, block = blocks
    rows = block // 2
    team = 2 * seq
    size = seq * block
    scale = HD ** (-0.5)

    def kernel(
        me_ref, core_ref, pair_ref, own_ref, other_ref, proj_ref, qkv_ref, att_ref, near_ref,
        h_ref, w_ref, own_x_ref, other_x_ref, keep_ref, send_ref, h_own_ref, h_other_ref,
        sums_ref, cols_ref, grads_ref, whole_ref, rows_ref,
    ):
        proj_rows = proj_ref[me_ref[0]]
        grad_mine, grad_near = 0.0, 0.0
        for at in range(count):
            where = slice(at * seq_len, (at + 1) * seq_len)
            away = (at + latents) % count
            away = slice(away * seq_len, (away + 1) * seq_len)
            lane = at % latents
            x = own_x_ref[0, lane] if at < latents else other_x_ref[0, lane]
            lane = slice(lane * seq_len, (lane + 1) * seq_len)
            grad_attn = own_ref[lane] if at < latents else other_ref[lane]
            grad_mine = grad_mine + dot_lt(att_ref[where], grad_attn)
            grad_near = grad_near + dot_lt(near_ref[away], grad_attn)
            grad_out = dot_rt(grad_attn, proj_rows).astype(BF16)
            pieces = [[], [], []]
            for head in range(group // HD):
                query, key, value = (
                    qkv_ref[where, part * group + head * HD : part * group + (head + 1) * HD]
                    for part in range(3)
                )
                grad_head = grad_out[:, head * HD : (head + 1) * HD]
                probs = softmax(query, key)
                grad_probs = dot_rt(grad_head, value)
                inner = jnp.sum(grad_probs * probs, axis=-1, keepdims=True)
                grad_scores = (probs * (grad_probs - inner)).astype(BF16)
                pieces[0].append((dot(grad_scores, key) * scale).astype(BF16))
                pieces[1].append((dot_lt(grad_scores, query) * scale).astype(BF16))
                pieces[2].append(dot_lt(probs.astype(BF16), grad_head).astype(BF16))
            grad_qkv = jnp.concatenate(sum(pieces, []), axis=1)
            grads_ref[where] = grad_qkv
            grad_h = dot_rt(grad_qkv, w_ref[...])
            norm = norm_parts(x.astype(F32))[0]
            sums_ref[at, 0:1] = jnp.sum(grad_h, axis=0, keepdims=True)
            sums_ref[at, 1:2] = jnp.sum(grad_h * norm, axis=0, keepdims=True)
            if at < latents:
                h_own_ref[lane] = grad_h
            else:
                h_other_ref[lane] = grad_h.astype(BF16)
        cols_ref[...] = jnp.sum(grads_ref[...].astype(F32), axis=0, keepdims=True)
        whole = dot_lt(h_ref[...], grads_ref[...]).astype(BF16)
        whole_ref[...] = whole.reshape(whole_ref.shape)
        half_rows = (high,) + rows_ref.shape[1:]
        rows_ref[pl.ds(core_ref[0] * high, high)] = grad_mine.reshape(half_rows)
        rows_ref[pl.ds((1 - core_ref[0]) * high, high)] = grad_near.reshape(half_rows)
        for to, out_ref in ((pair_ref[0], keep_ref), (1 - pair_ref[0], send_ref)):
            for second in range(high):
                ours = [whole_ref[first * high + second, to] for first in range(seq)]
                piece = rows_ref[second * 2 + to, core_ref[0]]
                beside = jnp.concatenate(
                    [piece[:, at * group : (at + 1) * group] for at in range(team)], axis=0
                )
                out_ref[second] = jnp.concatenate(
                    [jnp.concatenate(ours, axis=0), beside.astype(BF16)], axis=1
                )

    own_total = latents * seq_len
    outs = [
        ((high, size, columns + group), BF16),
        ((high, size, columns + group), BF16),
        ((own_total, width), F32),
        ((own_total, width), BF16),
        ((count, 2, width), F32),
        ((1, columns), F32),
    ]
    scratch = [
        ((total, columns), BF16),
        ((seq * high, 2, block, columns), BF16),
        ((2 * high, 2, rows, width), F32),
    ]
    return call(
        kernel, outs, me, core, pair, own_grad, other_grad, proj, qkv, attended, near, h_low,
        weight, own_x, other_x, scalars=3, scratch=scratch, us=12,
    )


def join_fc1(me, pair, pieces, high):
    rows, hidden = pieces[0].shape
    wide = hidden // (2 * high)
    team = len(pieces)

    def kernel(me_ref, pair_ref, *refs):
        ins, out_ref, held_ref = refs[:team], refs[team], refs[team + 1]
        for step, piece_ref in enumerate(ins):
            piece = piece_ref[...].astype(F32)
            turned = jnp.concatenate([piece[:, hidden // 2 :], piece[:, : hidden // 2]], axis=1)
            held_ref[jnp.bitwise_xor(me_ref[0], step)] = jnp.where(
                pair_ref[0] == 0, piece, turned
            )
        out = []
        for first in range(team // 2):
            for second in range(high):
                for side in range(2):
                    at = (side * high + second) * wide
                    for core in range(2):
                        out.append(held_ref[first * 2 + core][:, at : at + wide])
        out_ref[...] = jnp.concatenate(out, axis=1)

    outs = [((rows, team * hidden), F32)]
    return call(
        kernel, outs, me, pair, *pieces, scalars=2, scratch=[((team, rows, hidden), F32)], us=2
    )[0]


def join_qkv(me, pieces):
    rows, columns = pieces[0].shape
    group = columns // 3
    team = len(pieces)

    def kernel(me_ref, *refs):
        ins, out_ref, held_ref = refs[:team], refs[team], refs[team + 1]
        for step, piece_ref in enumerate(ins):
            held_ref[jnp.bitwise_xor(me_ref[0], step)] = piece_ref[...].astype(F32)
        out = [
            held_ref[member][:, part * group : (part + 1) * group]
            for part in range(3)
            for member in range(team)
        ]
        out_ref[...] = jnp.concatenate(out, axis=1)

    outs = [((rows, team * columns), F32)]
    return call(
        kernel, outs, me, *pieces, scalars=1, scratch=[((team, rows, columns), F32)], us=2
    )[0]


def local(
    shards,
    split,
    tokens,
    cond,
    w_ada,
    b_ada,
    w_qkv,
    b_query,
    b_value,
    w_proj,
    b_proj,
    w_fc1,
    b_fc1,
    w_fc2,
    b_fc2,
    cotangent,
):
    seq, fsdp = split
    link = Links(shards)
    low_bits = int(math.log2(fsdp))
    core_bit = [0]
    seq_bits = list(range(low_bits, int(math.log2(shards))))[::-1]
    pair_bit, high_bits = [1], list(range(2, low_bits))[::-1]
    team_bits = seq_bits + core_bit
    team = seq * 2
    rest = fsdp // 2
    high = rest // 2
    core, half, me = link.place(core_bit), link.place(seq_bits), link.place(team_bits)
    pair, spot = link.place(pair_bit), link.place(high_bits)
    latents, local_len, width = tokens.shape
    seq_len = seq * local_len
    rows = w_qkv.shape[0]
    hidden_rows = w_fc2.shape[0]
    hidden = hidden_rows * rest
    group = width // team
    columns = 3 * group
    count = 2 * latents
    chips = shards // 2

    direct = [jnp.concatenate([w_fc2, w_proj], axis=0)[None]]
    for bit in high_bits:
        direct.append(link.gather_step(direct[-1], bit))

    cond_float = cond.astype(F32)
    silu_cond = jax.nn.silu(cond_float).astype(BF16)
    mine = latents * rows
    cond_blocks = silu_cond.reshape(latents, seq, fsdp, rows)
    cond_blocks = link.pick(cond_blocks, half, 1).swapaxes(0, 1).reshape(fsdp, mine)
    small = 4 * rows + hidden_rows
    bias_row = sum(
        jnp.pad(bias[None], ((0, 0), (start, mine + small - start - bias.shape[0])))
        for start, bias in (
            (mine, b_query), (mine + rows, b_value), (mine + 2 * rows, b_proj),
            (mine + 3 * rows, b_fc2), (mine + 4 * rows, b_fc1),
        )
    )
    to_all = jnp.pad(cond_blocks, ((0, 0), (0, small))) + bias_row
    from_all = lax.all_to_all(to_all, "fsdp", 0, 0, tiled=True)
    all_cond = from_all[:, :mine].reshape(fsdp * latents, rows)
    biases = from_all[:, mine:]
    bias_q, bias_v = (
        lax.dynamic_slice_in_dim(
            biases[:, at * rows : (at + 1) * rows].reshape(1, -1), core * group, group, 1
        ).astype(F32)
        for at in range(2)
    )
    bias_qkv = jnp.concatenate([bias_q, jnp.zeros_like(bias_q), bias_v], axis=1)
    bias_fc1 = biases[:, 4 * rows :].reshape(high, 2, 2, hidden_rows)
    bias_fc1 = link.flip(link.pick(bias_fc1, core, 2).swapaxes(0, 1), pair_bit)
    bias_fc1 = bias_fc1.reshape(1, hidden).astype(F32)

    acts = jnp.stack([tokens, cotangent]).reshape(-1, 1, local_len, width)
    acts = interleave_call(acts, link.send(acts, seq_bits), half, jnp.int32(0))
    acts = acts.reshape(2, latents, seq_len, width)
    team_qkv = w_qkv.reshape(rows, 3, team, group).transpose(2, 0, 1, 3)
    team_fc1 = w_fc1.reshape(rows, seq, high, 2, 2, hidden_rows).transpose(3, 2, 1, 4, 0, 5)
    team_fc1 = link.flip(team_fc1, pair_bit).transpose(2, 3, 4, 0, 1, 5)
    team_part = jnp.concatenate(
        [team_qkv.reshape(team, rows, columns), team_fc1.reshape(team, rows, hidden)], axis=2
    )
    team_part = link.exchange(team_part, team_bits)
    part = dot(after(all_cond, team_part), w_ada)
    own_columns = (jnp.arange(shards) == link.index)[:, None] * b_ada.astype(F32)[None, :]
    part = after(part + own_columns.reshape(-1), direct[1])
    part = part.reshape(fsdp * latents, 2, 3 * width)
    team_qkv = team_part[:, :, :columns].reshape(1, seq, 2 * rows, columns)
    team_fc1 = team_part[:, :, columns:].reshape(1, seq, 2 * rows, hidden)
    steps = [team_qkv, link.gather_step(team_qkv, high_bits[0])]
    part = link.pick(part, core, 1) + link.send(link.pick(part, 1 - core, 1), core_bit)
    part = after(part, steps[1], acts)
    part = part.reshape(1, rest, count * 3 * width)
    part = jnp.broadcast_to(part, (seq, rest, count * 3 * width)).reshape(chips, -1)
    sent_part = part
    part = link.all_to_all(part, seq_bits + [*high_bits, *pair_bit])

    direct_own = direct[-1]
    direct_other = link.send(direct_own, pair_bit)
    for bit in high_bits[1:]:
        steps.append(link.gather_step(steps[-1], bit, (part,)))
    qkv_own = steps[-1]
    qkv_other = link.send(qkv_own, pair_bit)
    other_acts = link.send(acts, core_bit)
    fc1_steps = [after(team_fc1, steps[2])]
    for bit in high_bits:
        fc1_steps.append(link.gather_step(fc1_steps[-1], bit, (qkv_own,)))
    fc1_own = fc1_steps[-1]
    fc1_other = link.send(fc1_own, pair_bit)
    part = after(part, qkv_own, other_acts)
    modulation = jnp.sum(part, axis=0).reshape(2, latents, 3, width)
    full_proj = interleave_call(
        direct_own[:, None, hidden_rows:], direct_other[:, None, hidden_rows:], pair, spot
    )
    half_proj = full_proj
    full_proj = link.gather(full_proj.reshape(rest, rows, width), seq_bits, 0)
    full_proj = link.gather(full_proj, core_bit, 2).reshape(team, group, width)
    bias_out = link.gather(after(biases, qkv_own)[:, 2 * rows : 4 * rows], seq_bits, 0)
    bias_proj, bias_fc2 = (
        bias_out[:, :, at * rows : (at + 1) * rows].reshape(1, width).astype(F32) for at in range(2)
    )
    wide = max(width, hidden)
    feed_biases = jnp.concatenate(
        [
            jnp.pad(bias, ((0, 0), (0, wide - bias.shape[1])))
            for bias in (bias_proj, bias_fc1, bias_fc2 * (1.0 / team))
        ],
        axis=0,
    )

    mod, h_attn, qkv, attended, my_qkv = attend(
        core, pair, spot, modulation, link.send(modulation, core_bit), acts, other_acts,
        after(qkv_own, half_proj, fc1_own),
        qkv_other, bias_qkv,
    )

    near = link.send(attended, core_bit)
    far = link.send(attended, seq_bits)
    across = link.send(far, core_bit)
    (
        attn, mid, grad_h, other_h, keep_fc1, send_fc1, keep_fc2, send_fc2, branch, other_branch,
        grad_gate_mlp, sums_mlp,
    ) = feed(
        me, pair, spot, [attended, near, far, across], full_proj, feed_biases, acts, other_acts,
        mod, fc1_own, fc1_other, direct_own, direct_other,
    )
    grad_h = (grad_h + link.send(other_h, core_bit).astype(F32)).astype(BF16)
    there_h = link.send(grad_h, seq_bits)
    sent_fc2 = link.send(send_fc2, pair_bit)
    sent_fc1 = link.send(send_fc1, pair_bit)
    sent_branch = link.send(other_branch, core_bit)
    grad_mid, grad_attn, sums_mid = norm_backward(grad_h, there_h, mid, attn, acts, mod)
    other_attn = link.send(grad_attn, core_bit)
    grad_fc2 = after(keep_fc2, grad_attn).astype(F32) + sent_fc2.astype(F32)
    grad_fc2 = grad_fc2.astype(BF16).reshape(high, hidden_rows, width)
    keep_qkv, send_qkv, grad_h_attn, other_h_attn, sums_attn, sums_qkv = attend_back(
        me, core, pair, after(grad_attn, grad_fc2), other_attn, full_proj, qkv, attended, near,
        h_attn, my_qkv, acts, other_acts, (seq, high, 2 * rows),
    )

    late = jnp.concatenate([sums_attn, grad_gate_mlp], axis=1)
    late = late[:latents] + link.send(late[latents:], core_bit)
    late = late + link.send(late, seq_bits)
    grad_mod = jnp.concatenate([late[:, :2], sums_mid, late[:, 2:]], axis=1)
    grad_mod = grad_mod.reshape(1, -1, 128).astype(BF16)
    grad_mod = jnp.broadcast_to(grad_mod, (fsdp,) + grad_mod.shape[1:])
    sent_qkv = link.send(send_qkv, pair_bit)
    grad_qkv = after(keep_qkv, late).astype(F32) + sent_qkv.astype(F32)
    grad_qkv = grad_qkv.astype(BF16)
    grad_mod = after(grad_mod, grad_qkv)
    sent_mod = grad_mod
    grad_fc2 = link.scatter(grad_fc2, high_bits, (sent_mod,), (sums_attn,))
    grad_mod = lax.all_to_all(grad_mod, "fsdp", 0, 0, tiled=True)
    grad_mod = grad_mod.reshape(fsdp * latents, 6 * width)

    grad_silu = dot_rt(grad_mod, w_ada).reshape(1, fsdp, mine)
    grad_silu = jnp.broadcast_to(grad_silu, (seq, fsdp, mine)).reshape(shards, -1)
    grad_ada = dot_lt(all_cond, grad_mod)
    own_ada = b_ada.shape[0]
    grad_b_ada = lax.dynamic_slice_in_dim(grad_mod, link.index * own_ada, own_ada, 1)
    grad_b_ada = jnp.sum(grad_b_ada.astype(F32), axis=0)
    everyone = 1.0 / team
    sums_proj = jnp.sum(grad_attn.astype(F32), axis=0) * (1.0 / seq)
    sums_branch, sums_up = sums_mlp[0, :width] * everyone, sums_mlp[1, :hidden]
    sums_proj, sums_branch, sums_up, sums_qkv = after(
        (sums_proj, sums_branch, sums_up, sums_qkv), sent_mod
    )
    in_team = (jnp.arange(team) == me)[:, None]
    by_owner = [sums_branch.reshape(shards, rows), sums_proj.reshape(shards, rows)]
    for sums in (sums_qkv[:, :group], sums_qkv[:, 2 * group :]):
        by_owner.append(jnp.where(in_team, sums, 0.0).reshape(shards, rows))
    sums_up = link.flip(sums_up.reshape(2, high, hidden_rows), pair_bit).swapaxes(0, 1)
    sums_up = sums_up.reshape(1, rest, 1, hidden_rows)
    in_seq = jnp.arange(seq).reshape(seq, 1, 1, 1) == half
    in_core = jnp.arange(2).reshape(1, 1, 2, 1) == core
    by_owner.append(jnp.where(in_seq & in_core, sums_up, 0.0).reshape(shards, hidden_rows))
    tail = jnp.concatenate([grad_silu] + by_owner, axis=1)
    tail = lax.all_to_all(tail, AXES, 0, 0, tiled=True)
    grad_fc1 = after(keep_fc1, sums_attn).astype(F32) + sent_fc1.astype(F32)
    grad_fc1 = link.scatter(grad_fc1.astype(BF16), high_bits, (tail,), (grad_qkv,)).astype(BF16)
    grad_fc1 = link.exchange_pieces(grad_fc1.reshape(team, rows, hidden), team_bits)
    grad_fc1 = join_fc1(me, pair, grad_fc1, high)
    grad_qkv = link.scatter(grad_qkv, high_bits, (tail,))
    grad_proj = grad_qkv[:, columns:].reshape(team, rows, group)
    grad_proj = jnp.concatenate([grad_proj[at] for at in range(team)], axis=1)
    grad_qkv = grad_qkv[:, :columns].astype(BF16).reshape(team, rows, columns)
    grad_qkv = join_qkv(me, link.exchange_pieces(grad_qkv, team_bits))

    def own_rows(value):
        value = value.reshape(latents, seq_len, -1)
        return lax.dynamic_slice_in_dim(value, half * local_len, local_len, 1)

    branch = after(branch, other_attn) + sent_branch.astype(F32)
    grad_h_attn = after(grad_h_attn, sent_mod) + link.send(other_h_attn, core_bit).astype(F32)
    both = jnp.stack([branch, grad_h_attn]).reshape(2, latents, seq, local_len, width)
    both = link.scatter(jnp.moveaxis(both, 2, 0), seq_bits, (tail,))
    output = (own_rows(mid) + mod[:latents, 5:6] * both[0]).astype(BF16)
    norm, rate = norm_parts(tokens.astype(F32))
    grad_tokens = norm_back(norm, rate, both[1] * (1.0 + mod[:latents, 1:2]))
    grad_tokens = (own_rows(grad_mid) + grad_tokens).astype(BF16)

    grad_silu = tail[:, :mine].reshape(shards, latents, rows).swapaxes(0, 1)
    grad_silu = grad_silu.reshape(latents, width)
    silu_back = jax.vjp(jax.nn.silu, cond_float)[1]
    grad_cond = silu_back(grad_silu)[0].astype(BF16)
    sums = jnp.sum(tail[:, mine:], axis=0)
    return (
        output,
        grad_tokens,
        grad_cond,
        grad_ada,
        grad_b_ada,
        grad_qkv,
        sums[2 * rows : 3 * rows],
        sums[3 * rows : 4 * rows],
        grad_proj,
        sums[rows : 2 * rows],
        grad_fc1,
        sums[4 * rows :],
        grad_fc2,
        sums[:rows],
    )


def solution(mesh):
    seq, fsdp = mesh.shape["seq"], mesh.shape["fsdp"]
    act = P("fsdp", "seq", None)
    matrix = P(AXES, None)
    vector = P(AXES)
    cond = P("fsdp", None)
    in_specs = (
        act, cond, matrix, vector, matrix, vector, vector, matrix, vector, matrix, vector, matrix,
        vector, act,
    )
    out_specs = (
        act, act, cond, matrix, vector, matrix, vector, vector, matrix, vector, matrix, vector,
        matrix, vector,
    )

    def layer(*args):
        return local(seq * fsdp, (seq, fsdp), *args)

    return jax.shard_map(layer, mesh=mesh, in_specs=in_specs, out_specs=out_specs, check_vma=False)
```

```python
import math

import jax
import jax.numpy as jnp
from jax import lax
from jax.experimental import pallas as pl
from jax.experimental.pallas import tpu as pltpu
from jax.sharding import PartitionSpec as P

HD = 64
AXES = ("seq", "fsdp")
F32 = jnp.float32
BF16 = jnp.bfloat16
VMEM_SPEC = pl.BlockSpec(memory_space=pltpu.VMEM)
SMEM_SPEC = pl.BlockSpec(memory_space=pltpu.SMEM)


def contract(left, right, left_dim, right_dim):
    return lax.dot_general(
        left, right, (((left_dim,), (right_dim,)), ((), ())), preferred_element_type=F32
    )


def dot(left, right):
    return contract(left, right, 1, 0)


def dot_rt(left, right):
    return contract(left, right, 1, 1)


def dot_lt(left, right):
    return contract(left, right, 0, 0)


def norm_parts(value):
    centre = value - jnp.mean(value, axis=-1, keepdims=True)
    variance = jnp.mean(centre * centre, axis=-1, keepdims=True)
    scale = lax.rsqrt(variance + 1e-06)
    return centre * scale, scale


def norm_back(norm, rate, grad):
    inner = jnp.mean(grad * norm, axis=-1, keepdims=True)
    return rate * (grad - jnp.mean(grad, axis=-1, keepdims=True) - norm * inner)


def after(value, *earlier):
    return lax.optimization_barrier((value,) + earlier)[0]


class Links:
    def __init__(self, devices):
        self.devices = devices
        self.index = lax.axis_index(AXES)

    def place(self, bits):
        spot = jnp.int32(0)
        for bit in bits:
            spot = spot * 2 + ((self.index >> bit) & 1)
        return spot

    def mask(self, bits, step):
        total = 0
        for at, bit in enumerate(reversed(bits)):
            total |= ((step >> at) & 1) << bit
        return total

    def groups(self, bits):
        steps = [self.mask(bits, step) for step in range(1 << len(bits))]
        return [
            [base | step for step in steps] for base in range(self.devices) if not base & steps[-1]
        ]

    def send(self, value, bits, step=1):
        mask = self.mask(bits, step)
        return lax.ppermute(value, AXES, [(i, i ^ mask) for i in range(self.devices)])

    def all_to_all(self, value, bits):
        return lax.all_to_all(
            value, AXES, 0, 0, tiled=True, axis_index_groups=self.groups(bits)
        )

    def flip(self, value, bits):
        shape = value.shape
        value = value.reshape((2,) * len(bits) + shape[1:])
        for axis, bit in enumerate(bits):
            first, second = jnp.split(value, 2, axis)
            turned = jnp.concatenate([second, first], axis)
            value = jnp.where(self.place([bit]) == 0, value, turned)
        return value.reshape(shape)

    def gather_step(self, value, bit, earlier=()):
        part = self.send(value, [bit])
        if earlier:
            value = after(value, *earlier)
        return jnp.concatenate([value, part], 0)

    def exchange(self, value, bits):
        value = self.flip(value, bits)
        parts = [value[:1]]
        for step in range(1, 1 << len(bits)):
            parts.append(self.send(value[step : step + 1], bits, step))
        return self.flip(jnp.concatenate(parts, 0), bits)

    def exchange_pieces(self, value, bits):
        spot = self.place(bits)
        parts = [self.pick(value, spot)]
        for step in range(1, 1 << len(bits)):
            parts.append(self.send(self.pick(value, spot ^ step), bits, step))
        return parts

    def gather(self, value, bits, axis):
        spot = self.place(bits)
        part = self.send(value, bits)
        shape = value.shape[:axis] + (2,) + value.shape[axis:]
        out = jnp.zeros(shape, value.dtype)
        out = lax.dynamic_update_index_in_dim(out, value, spot, axis)
        return lax.dynamic_update_index_in_dim(out, part, 1 - spot, axis)

    def pick(self, value, spot, axis=0):
        return lax.dynamic_index_in_dim(value, spot, axis, keepdims=False)

    def scatter(self, value, bits, earlier=(), first=()):
        for bit in reversed(bits):
            spot = self.place([bit])
            value = value.reshape((-1, 2) + value.shape[1:])
            part = self.send(self.pick(value, 1 - spot, 1).astype(BF16), [bit])
            value = self.pick(value, spot, 1)
            ready = earlier if bit == bits[0] else first
            if ready:
                value = after(value, *ready)
            value = value.astype(F32) + part.astype(F32)
            if bit != bits[0]:
                value = value.astype(BF16)
        return value[0]


def call(kernel, outs, *args, scalars=0, scratch=(), us=5):
    arrays = [jnp.reshape(arg, 1) for arg in args[:scalars]] + list(args[scalars:])
    return pl.pallas_call(
        kernel,
        out_shape=[jax.ShapeDtypeStruct(shape, dtype) for shape, dtype in outs],
        in_specs=[SMEM_SPEC] * scalars + [VMEM_SPEC] * (len(args) - scalars),
        out_specs=[VMEM_SPEC] * len(outs),
        scratch_shapes=[pltpu.VMEM(shape, dtype) for shape, dtype in scratch],
        compiler_params=pltpu.CompilerParams(vmem_limit_bytes=48 * 2**20),
        cost_estimate=pl.CostEstimate(
            flops=us * 10**8, bytes_accessed=us * 3 * 10**5, transcendentals=0
        ),
    )(*arrays)


def step_order(count):
    order = [0]
    while count > 1:
        count //= 2
        order = order + [at ^ count for at in order]
    return order


def interleave(own_ref, other_ref, out_ref, pair, high, swap=False):
    outer, inner, rows, cols = own_ref.shape
    for first, away in enumerate(step_order(outer)):
        to = jnp.bitwise_xor(high, away)
        for second in range(inner):
            out_ref[second, to, pair] = own_ref[first, second]
            piece = other_ref[first, second]
            if swap:
                piece = jnp.concatenate([piece[:, cols // 2 :], piece[:, : cols // 2]], axis=1)
            out_ref[second, to, 1 - pair] = piece


def interleave_call(own, other, pair, high):
    outer, inner, rows, cols = own.shape

    def kernel(pair_ref, high_ref, own_ref, other_ref, out_ref):
        interleave(own_ref, other_ref, out_ref, pair_ref[0], high_ref[0])

    shape = (inner, outer, 2, rows, cols)
    return call(kernel, [(shape, own.dtype)], pair, high, own, other, scalars=2, us=2)[0]


def attend(core, pair, high, mine, there, own_x, other_x, own_w, other_w, bias):
    latents, seq_len, width = own_x.shape[1:]
    count = 2 * latents
    columns = own_w.shape[3]
    group = columns // 3
    total = count * seq_len

    def kernel(
        core_ref, pair_ref, high_ref, mine_ref, there_ref, own_ref, other_ref, own_w_ref,
        other_w_ref, b_ref, mod_ref, h_ref, qkv_ref, out_ref, w_out_ref, w_ref,
    ):
        interleave(own_w_ref, other_w_ref, w_ref, pair_ref[0], high_ref[0])
        weight = w_ref[...].reshape(width, columns)
        w_out_ref[...] = weight
        core_at = core_ref[0]
        for side in range(2):
            row = jnp.bitwise_xor(core_at, side)
            for latent in range(latents):
                one, two = mine_ref[row, latent], there_ref[row, latent]
                first = jnp.where(core_at == 0, one, two)
                second = jnp.where(core_at == 0, two, one)
                mod_ref[side * latents + latent, 0:3] = first
                mod_ref[side * latents + latent, 3:6] = second
        for at in range(count):
            where = slice(at * seq_len, (at + 1) * seq_len)
            x = own_ref[0, at] if at < latents else other_ref[0, at - latents]
            norm = norm_parts(x.astype(F32))[0]
            shift, scale = mod_ref[at, 0:1], mod_ref[at, 1:2]
            h_low = (norm * (1.0 + scale) + shift).astype(BF16)
            h_ref[where] = h_low
            qkv = (dot(h_low, weight) + b_ref[...]).astype(BF16)
            qkv_ref[where] = qkv
            pieces = []
            for head in range(group // HD):
                query, key, value = (
                    qkv[:, part * group + head * HD : part * group + (head + 1) * HD]
                    for part in range(3)
                )
                probs = softmax(query, key).astype(BF16)
                pieces.append(dot(probs, value).astype(BF16))
            out_ref[where] = jnp.concatenate(pieces, axis=1)

    outs = [
        ((count, 6, width), F32),
        ((total, width), BF16),
        ((total, columns), BF16),
        ((total, group), BF16),
        ((width, columns), BF16),
    ]
    placed = (own_w.shape[1], own_w.shape[0], 2) + own_w.shape[2:]
    return call(
        kernel, outs, core, pair, high, mine, there, own_x, other_x, own_w, other_w, bias,
        scalars=3, scratch=[(placed, BF16)], us=6,
    )


def softmax(query, key):
    scores = dot_rt(query, key) * HD ** (-0.5)
    top = jnp.max(scores, axis=-1, keepdims=True)
    log_total = top + jnp.log(jnp.sum(jnp.exp(scores - top), axis=-1, keepdims=True))
    return jnp.exp(scores - log_total)


def feed(me, pair, high, pieces, proj, biases, own_x, other_x, mod, own_1, other_1, own_2, other_2):
    latents, seq_len, width = own_x.shape[1:]
    count = 2 * latents
    total = count * seq_len
    members = len(pieces)
    outer, seq, block, hidden = own_1.shape
    front = hidden // 2
    hidden_rows = hidden // (2 * outer)

    def kernel(me_ref, pair_ref, high_ref, *refs):
        piece_refs, refs = refs[:members], refs[members:]
        (
            proj_ref, bias_ref, own_ref, other_ref, mod_ref, own_1_ref, other_1_ref, own_2_ref,
            other_2_ref, attn_ref, mid_ref, h_own_ref, h_other_ref, keep_1_ref, send_1_ref,
            keep_2_ref, send_2_ref, out_own_ref, out_other_ref, gate_ref, sums_ref,
            fc1_ref, fc2_ref, h_ref, act_ref, up_ref, branch_ref, whole_ref,
        ) = refs
        interleave(own_1_ref, other_1_ref, fc1_ref, pair_ref[0], high_ref[0], swap=True)
        for at, away in enumerate(step_order(outer)):
            to = jnp.bitwise_xor(high_ref[0], away)
            fc2_ref[0, to] = own_2_ref[at, :hidden_rows]
            fc2_ref[1, to] = other_2_ref[at, :hidden_rows]
        fc1 = fc1_ref[...].reshape(width, hidden)
        fc2 = fc2_ref[...].reshape(hidden, width)
        sums_up, sums_branch = 0.0, 0.0
        for at in range(count):
            where = slice(at * seq_len, (at + 1) * seq_len)
            near = at % latents
            lane = slice(near * seq_len, (near + 1) * seq_len)
            away = (at + latents) % count
            away = slice(away * seq_len, (away + 1) * seq_len)
            x_ref = own_ref if at < latents else other_ref
            x, cotangent = x_ref[0, near].astype(F32), x_ref[1, near].astype(F32)
            mods = [mod_ref[at, part : part + 1] for part in range(6)]
            attn = bias_ref[0:1, :width]
            for step, piece_ref in enumerate(piece_refs):
                piece = piece_ref[away if step % 2 else where]
                attn = attn + dot(piece, proj_ref[jnp.bitwise_xor(me_ref[0], step)])
            mid = x + mods[2] * attn
            if at < latents:
                attn_ref[where] = attn
                mid_ref[where] = mid
            h_low = (norm_parts(mid)[0] * (1.0 + mods[4]) + mods[3]).astype(BF16)
            h_ref[where] = h_low
            up = dot(h_low, fc1) + bias_ref[1:2, :hidden]
            square = up * up
            bend = jnp.tanh(0.7978845608028654 * up * (1.0 + 0.044715 * square))
            act = (0.5 * up * (1.0 + bend)).astype(BF16)
            act_ref[where] = act
            slope = 0.7978845608028654 * (1.0 + 0.134145 * square)
            slope = 0.5 * (1.0 + bend) + 0.5 * up * (1.0 - bend * bend) * slope
            grad_branch = (mods[5] * cotangent).astype(BF16)
            branch_ref[where] = grad_branch
            grad_up = (slope * dot_rt(grad_branch, fc2)).astype(BF16)
            up_ref[where] = grad_up
            grad_h = dot_rt(grad_up, fc1)
            out = dot(act, fc2) + bias_ref[2:3, :width]
            gate_ref[at] = jnp.sum(cotangent * out, axis=0, keepdims=True)
            if at < latents:
                h_own_ref[lane] = grad_h
                out_own_ref[lane] = out
            else:
                h_other_ref[lane] = grad_h.astype(BF16)
                out_other_ref[lane] = out.astype(BF16)
            sums_branch = sums_branch + jnp.sum(
                grad_branch.astype(F32), axis=0, keepdims=True
            )
            sums_up = sums_up + jnp.sum(grad_up.astype(F32), axis=0, keepdims=True)
        sums_ref[0:1, :width] = sums_branch
        sums_ref[1:2, :hidden] = sums_up
        grad_2 = dot_lt(act_ref[...], branch_ref[...]).astype(BF16)
        keep_2_ref[...] = grad_2[:front]
        send_2_ref[...] = grad_2[front:]
        whole_ref[...] = dot_lt(h_ref[...], up_ref[...]).astype(BF16).reshape(whole_ref.shape)
        for first in range(seq):
            for second in range(outer):
                lane = slice(first * block, (first + 1) * block)
                at = first * outer + second
                keep_1_ref[second, lane] = whole_ref[at, pair_ref[0]]
                piece = whole_ref[at, 1 - pair_ref[0]]
                send_1_ref[second, lane] = jnp.concatenate(
                    [piece[:, front:], piece[:, :front]], axis=1
                )

    own_total = latents * seq_len
    wide = max(width, hidden)
    outs = [
        ((own_total, width), F32),
        ((own_total, width), F32),
        ((own_total, width), F32),
        ((own_total, width), BF16),
        ((outer, seq * block, hidden), BF16),
        ((outer, seq * block, hidden), BF16),
        ((front, width), BF16),
        ((front, width), BF16),
        ((own_total, width), F32),
        ((own_total, width), BF16),
        ((count, 1, width), F32),
        ((2, wide), F32),
    ]
    scratch = [
        ((seq, outer, 2, block, hidden), BF16),
        ((2, outer, hidden_rows, width), BF16),
        ((total, width), BF16),
        ((total, hidden), BF16),
        ((total, hidden), BF16),
        ((total, width), BF16),
        ((seq * outer, 2, block, hidden), BF16),
    ]
    args = pieces + [proj, biases, own_x, other_x, mod, own_1, other_1, own_2, other_2]
    return call(kernel, outs, me, pair, high, *args, scalars=3, scratch=scratch, us=12)


def norm_backward(mine, there, mid, attn, own_x, mod):
    latents, seq_len, width = own_x.shape[1:]

    def kernel(
        mine_ref, there_ref, mid_ref, attn_ref, x_ref, mod_ref, grad_ref, low_ref, sums_ref
    ):
        for at in range(latents):
            where = slice(at * seq_len, (at + 1) * seq_len)
            grad_h = mine_ref[where].astype(F32) + there_ref[where].astype(F32)
            norm, rate = norm_parts(mid_ref[where])
            grad = x_ref[1, at].astype(F32) + norm_back(
                norm, rate, grad_h * (1.0 + mod_ref[at, 4:5])
            )
            grad_ref[where] = grad
            low_ref[where] = (mod_ref[at, 2:3] * grad).astype(BF16)
            sums_ref[at, 0:1] = jnp.sum(grad * attn_ref[where], axis=0, keepdims=True)
            sums_ref[at, 1:2] = jnp.sum(grad_h, axis=0, keepdims=True)
            sums_ref[at, 2:3] = jnp.sum(grad_h * norm, axis=0, keepdims=True)

    outs = [
        ((latents * seq_len, width), F32),
        ((latents * seq_len, width), BF16),
        ((latents, 3, width), F32),
    ]
    return call(kernel, outs, mine, there, mid, attn, own_x, mod, us=3)


def attend_back(
    me, core, pair, own_grad, other_grad, proj, qkv, attended, near, h_low, weight, own_x, other_x,
    blocks,
):
    latents, seq_len, width = own_x.shape[1:]
    count = 2 * latents
    total, columns = qkv.shape
    group = columns // 3
    seq, high, block = blocks
    rows = block // 2
    team = 2 * seq
    size = seq * block
    scale = HD ** (-0.5)

    def kernel(
        me_ref, core_ref, pair_ref, own_ref, other_ref, proj_ref, qkv_ref, att_ref, near_ref,
        h_ref, w_ref, own_x_ref, other_x_ref, keep_ref, send_ref, h_own_ref, h_other_ref,
        sums_ref, cols_ref, grads_ref, whole_ref, rows_ref,
    ):
        proj_rows = proj_ref[me_ref[0]]
        grad_mine, grad_near = 0.0, 0.0
        for at in range(count):
            where = slice(at * seq_len, (at + 1) * seq_len)
            away = (at + latents) % count
            away = slice(away * seq_len, (away + 1) * seq_len)
            lane = at % latents
            x = own_x_ref[0, lane] if at < latents else other_x_ref[0, lane]
            lane = slice(lane * seq_len, (lane + 1) * seq_len)
            grad_attn = own_ref[lane] if at < latents else other_ref[lane]
            grad_mine = grad_mine + dot_lt(att_ref[where], grad_attn)
            grad_near = grad_near + dot_lt(near_ref[away], grad_attn)
            grad_out = dot_rt(grad_attn, proj_rows).astype(BF16)
            pieces = [[], [], []]
            for head in range(group // HD):
                query, key, value = (
                    qkv_ref[where, part * group + head * HD : part * group + (head + 1) * HD]
                    for part in range(3)
                )
                grad_head = grad_out[:, head * HD : (head + 1) * HD]
                probs = softmax(query, key)
                grad_probs = dot_rt(grad_head, value)
                inner = jnp.sum(grad_probs * probs, axis=-1, keepdims=True)
                grad_scores = (probs * (grad_probs - inner)).astype(BF16)
                pieces[0].append((dot(grad_scores, key) * scale).astype(BF16))
                pieces[1].append((dot_lt(grad_scores, query) * scale).astype(BF16))
                pieces[2].append(dot_lt(probs.astype(BF16), grad_head).astype(BF16))
            grad_qkv = jnp.concatenate(sum(pieces, []), axis=1)
            grads_ref[where] = grad_qkv
            grad_h = dot_rt(grad_qkv, w_ref[...])
            norm = norm_parts(x.astype(F32))[0]
            sums_ref[at, 0:1] = jnp.sum(grad_h, axis=0, keepdims=True)
            sums_ref[at, 1:2] = jnp.sum(grad_h * norm, axis=0, keepdims=True)
            if at < latents:
                h_own_ref[lane] = grad_h
            else:
                h_other_ref[lane] = grad_h.astype(BF16)
        cols_ref[...] = jnp.sum(grads_ref[...].astype(F32), axis=0, keepdims=True)
        whole = dot_lt(h_ref[...], grads_ref[...]).astype(BF16)
        whole_ref[...] = whole.reshape(whole_ref.shape)
        half_rows = (high,) + rows_ref.shape[1:]
        rows_ref[pl.ds(core_ref[0] * high, high)] = grad_mine.reshape(half_rows)
        rows_ref[pl.ds((1 - core_ref[0]) * high, high)] = grad_near.reshape(half_rows)
        for to, out_ref in ((pair_ref[0], keep_ref), (1 - pair_ref[0], send_ref)):
            for second in range(high):
                ours = [whole_ref[first * high + second, to] for first in range(seq)]
                piece = rows_ref[second * 2 + to, core_ref[0]]
                beside = jnp.concatenate(
                    [piece[:, at * group : (at + 1) * group] for at in range(team)], axis=0
                )
                out_ref[second] = jnp.concatenate(
                    [jnp.concatenate(ours, axis=0), beside.astype(BF16)], axis=1
                )

    own_total = latents * seq_len
    outs = [
        ((high, size, columns + group), BF16),
        ((high, size, columns + group), BF16),
        ((own_total, width), F32),
        ((own_total, width), BF16),
        ((count, 2, width), F32),
        ((1, columns), F32),
    ]
    scratch = [
        ((total, columns), BF16),
        ((seq * high, 2, block, columns), BF16),
        ((2 * high, 2, rows, width), F32),
    ]
    return call(
        kernel, outs, me, core, pair, own_grad, other_grad, proj, qkv, attended, near, h_low,
        weight, own_x, other_x, scalars=3, scratch=scratch, us=12,
    )


def join_fc1(me, pair, pieces, high):
    rows, hidden = pieces[0].shape
    wide = hidden // (2 * high)
    team = len(pieces)

    def kernel(me_ref, pair_ref, *refs):
        ins, out_ref, held_ref = refs[:team], refs[team], refs[team + 1]
        for step, piece_ref in enumerate(ins):
            piece = piece_ref[...].astype(F32)
            turned = jnp.concatenate([piece[:, hidden // 2 :], piece[:, : hidden // 2]], axis=1)
            held_ref[jnp.bitwise_xor(me_ref[0], step)] = jnp.where(
                pair_ref[0] == 0, piece, turned
            )
        out = []
        for first in range(team // 2):
            for second in range(high):
                for side in range(2):
                    at = (side * high + second) * wide
                    for core in range(2):
                        out.append(held_ref[first * 2 + core][:, at : at + wide])
        out_ref[...] = jnp.concatenate(out, axis=1)

    outs = [((rows, team * hidden), F32)]
    return call(
        kernel, outs, me, pair, *pieces, scalars=2, scratch=[((team, rows, hidden), F32)], us=2
    )[0]


def join_qkv(me, pieces):
    rows, columns = pieces[0].shape
    group = columns // 3
    team = len(pieces)

    def kernel(me_ref, *refs):
        ins, out_ref, held_ref = refs[:team], refs[team], refs[team + 1]
        for step, piece_ref in enumerate(ins):
            held_ref[jnp.bitwise_xor(me_ref[0], step)] = piece_ref[...].astype(F32)
        out = [
            held_ref[member][:, part * group : (part + 1) * group]
            for part in range(3)
            for member in range(team)
        ]
        out_ref[...] = jnp.concatenate(out, axis=1)

    outs = [((rows, team * columns), F32)]
    return call(
        kernel, outs, me, *pieces, scalars=1, scratch=[((team, rows, columns), F32)], us=2
    )[0]


def local(
    shards,
    split,
    tokens,
    cond,
    w_ada,
    b_ada,
    w_qkv,
    b_query,
    b_value,
    w_proj,
    b_proj,
    w_fc1,
    b_fc1,
    w_fc2,
    b_fc2,
    cotangent,
):
    seq, fsdp = split
    link = Links(shards)
    low_bits = int(math.log2(fsdp))
    core_bit = [0]
    seq_bits = list(range(low_bits, int(math.log2(shards))))[::-1]
    pair_bit, high_bits = [1], list(range(2, low_bits))[::-1]
    team_bits = seq_bits + core_bit
    team = seq * 2
    rest = fsdp // 2
    high = rest // 2
    core, half, me = link.place(core_bit), link.place(seq_bits), link.place(team_bits)
    pair, spot = link.place(pair_bit), link.place(high_bits)
    latents, local_len, width = tokens.shape
    seq_len = seq * local_len
    rows = w_qkv.shape[0]
    hidden_rows = w_fc2.shape[0]
    hidden = hidden_rows * rest
    group = width // team
    columns = 3 * group
    count = 2 * latents
    chips = shards // 2

    direct = [jnp.concatenate([w_fc2, w_proj], axis=0)[None]]
    for bit in high_bits:
        direct.append(link.gather_step(direct[-1], bit))

    cond_float = cond.astype(F32)
    silu_cond = jax.nn.silu(cond_float).astype(BF16)
    mine = latents * rows
    cond_blocks = silu_cond.reshape(latents, seq, fsdp, rows)
    cond_blocks = link.pick(cond_blocks, half, 1).swapaxes(0, 1).reshape(fsdp, mine)
    small = 4 * rows + hidden_rows
    bias_row = sum(
        jnp.pad(bias[None], ((0, 0), (start, mine + small - start - bias.shape[0])))
        for start, bias in (
            (mine, b_query), (mine + rows, b_value), (mine + 2 * rows, b_proj),
            (mine + 3 * rows, b_fc2), (mine + 4 * rows, b_fc1),
        )
    )
    to_all = jnp.pad(cond_blocks, ((0, 0), (0, small))) + bias_row
    from_all = lax.all_to_all(to_all, "fsdp", 0, 0, tiled=True)
    all_cond = from_all[:, :mine].reshape(fsdp * latents, rows)
    biases = from_all[:, mine:]
    bias_q, bias_v = (
        lax.dynamic_slice_in_dim(
            biases[:, at * rows : (at + 1) * rows].reshape(1, -1), core * group, group, 1
        ).astype(F32)
        for at in range(2)
    )
    bias_qkv = jnp.concatenate([bias_q, jnp.zeros_like(bias_q), bias_v], axis=1)
    bias_fc1 = biases[:, 4 * rows :].reshape(high, 2, 2, hidden_rows)
    bias_fc1 = link.flip(link.pick(bias_fc1, core, 2).swapaxes(0, 1), pair_bit)
    bias_fc1 = bias_fc1.reshape(1, hidden).astype(F32)

    acts = jnp.stack([tokens, cotangent]).reshape(-1, 1, local_len, width)
    acts = interleave_call(acts, link.send(acts, seq_bits), half, jnp.int32(0))
    acts = acts.reshape(2, latents, seq_len, width)
    team_qkv = w_qkv.reshape(rows, 3, team, group).transpose(2, 0, 1, 3)
    team_fc1 = w_fc1.reshape(rows, seq, high, 2, 2, hidden_rows).transpose(3, 2, 1, 4, 0, 5)
    team_fc1 = link.flip(team_fc1, pair_bit).transpose(2, 3, 4, 0, 1, 5)
    team_part = jnp.concatenate(
        [team_qkv.reshape(team, rows, columns), team_fc1.reshape(team, rows, hidden)], axis=2
    )
    team_part = link.exchange(team_part, team_bits)
    part = dot(after(all_cond, team_part), w_ada)
    own_columns = (jnp.arange(shards) == link.index)[:, None] * b_ada.astype(F32)[None, :]
    part = after(part + own_columns.reshape(-1), direct[1])
    part = part.reshape(fsdp * latents, 2, 3 * width)
    team_qkv = team_part[:, :, :columns].reshape(1, seq, 2 * rows, columns)
    team_fc1 = team_part[:, :, columns:].reshape(1, seq, 2 * rows, hidden)
    steps = [team_qkv, link.gather_step(team_qkv, high_bits[0])]
    part = link.pick(part, core, 1) + link.send(link.pick(part, 1 - core, 1), core_bit)
    part = after(part, steps[1], acts)
    part = part.reshape(1, rest, count * 3 * width)
    part = jnp.broadcast_to(part, (seq, rest, count * 3 * width)).reshape(chips, -1)
    sent_part = part
    part = link.all_to_all(part, seq_bits + [*high_bits, *pair_bit])

    direct_own = direct[-1]
    direct_other = link.send(direct_own, pair_bit)
    for bit in high_bits[1:]:
        steps.append(link.gather_step(steps[-1], bit, (part,)))
    qkv_own = steps[-1]
    qkv_other = link.send(qkv_own, pair_bit)
    other_acts = link.send(acts, core_bit)
    fc1_steps = [after(team_fc1, steps[1])]
    for bit in high_bits:
        fc1_steps.append(link.gather_step(fc1_steps[-1], bit, (qkv_own,)))
    fc1_own = fc1_steps[-1]
    fc1_other = link.send(fc1_own, pair_bit)
    part = after(part, qkv_own, other_acts)
    modulation = jnp.sum(part, axis=0).reshape(2, latents, 3, width)
    full_proj = interleave_call(
        direct_own[:, None, hidden_rows:], direct_other[:, None, hidden_rows:], pair, spot
    )
    half_proj = full_proj
    full_proj = link.gather(full_proj.reshape(rest, rows, width), seq_bits, 0)
    full_proj = link.gather(full_proj, core_bit, 2).reshape(team, group, width)
    mod, h_attn, qkv, attended, my_qkv = attend(
        core, pair, spot, modulation, link.send(modulation, core_bit), acts, other_acts,
        after(qkv_own, half_proj, fc1_own),
        qkv_other, bias_qkv,
    )

    bias_out = link.gather(after(biases, attended)[:, 2 * rows : 4 * rows], seq_bits, 0)
    bias_proj, bias_fc2 = (
        bias_out[:, :, at * rows : (at + 1) * rows].reshape(1, width).astype(F32) for at in range(2)
    )
    wide = max(width, hidden)
    feed_biases = jnp.concatenate(
        [
            jnp.pad(bias, ((0, 0), (0, wide - bias.shape[1])))
            for bias in (bias_proj, bias_fc1, bias_fc2 * (1.0 / team))
        ],
        axis=0,
    )

    near = link.send(attended, core_bit)
    far = link.send(attended, seq_bits)
    across = link.send(far, core_bit)
    (
        attn, mid, grad_h, other_h, keep_fc1, send_fc1, keep_fc2, send_fc2, branch, other_branch,
        grad_gate_mlp, sums_mlp,
    ) = feed(
        me, pair, spot, [attended, near, far, across], full_proj, feed_biases, acts, other_acts,
        mod, fc1_own, fc1_other, direct_own, direct_other,
    )
    grad_h = (grad_h + link.send(other_h, core_bit).astype(F32)).astype(BF16)
    there_h = link.send(grad_h, seq_bits)
    sent_fc2 = link.send(send_fc2, pair_bit)
    sent_fc1 = link.send(send_fc1, pair_bit)
    sent_branch = link.send(other_branch, core_bit)
    grad_mid, grad_attn, sums_mid = norm_backward(grad_h, there_h, mid, attn, acts, mod)
    other_attn = link.send(grad_attn, core_bit)
    grad_fc2 = after(keep_fc2, grad_attn).astype(F32) + sent_fc2.astype(F32)
    grad_fc2 = grad_fc2.astype(BF16).reshape(high, hidden_rows, width)
    keep_qkv, send_qkv, grad_h_attn, other_h_attn, sums_attn, sums_qkv = attend_back(
        me, core, pair, after(grad_attn, grad_fc2), other_attn, full_proj, qkv, attended, near,
        h_attn, my_qkv, acts, other_acts, (seq, high, 2 * rows),
    )

    late = jnp.concatenate([sums_attn, grad_gate_mlp], axis=1)
    late = late[:latents] + link.send(late[latents:], core_bit)
    late = late + link.send(late, seq_bits)
    grad_mod = jnp.concatenate([late[:, :2], sums_mid, late[:, 2:]], axis=1)
    grad_mod = grad_mod.reshape(1, -1, 128).astype(BF16)
    grad_mod = jnp.broadcast_to(grad_mod, (fsdp,) + grad_mod.shape[1:])
    sent_qkv = link.send(send_qkv, pair_bit)
    grad_qkv = after(keep_qkv, late).astype(F32) + sent_qkv.astype(F32)
    grad_qkv = grad_qkv.astype(BF16)
    grad_mod = after(grad_mod, grad_qkv)
    sent_mod = grad_mod
    grad_fc2 = link.scatter(grad_fc2, high_bits, (sent_mod,), (sums_attn,))
    grad_mod = lax.all_to_all(grad_mod, "fsdp", 0, 0, tiled=True)
    grad_mod = grad_mod.reshape(fsdp * latents, 6 * width)

    grad_silu = dot_rt(grad_mod, w_ada).reshape(1, fsdp, mine)
    grad_silu = jnp.broadcast_to(grad_silu, (seq, fsdp, mine)).reshape(shards, -1)
    grad_ada = dot_lt(all_cond, grad_mod)
    own_ada = b_ada.shape[0]
    grad_b_ada = lax.dynamic_slice_in_dim(grad_mod, link.index * own_ada, own_ada, 1)
    grad_b_ada = jnp.sum(grad_b_ada.astype(F32), axis=0)
    everyone = 1.0 / team
    sums_proj = jnp.sum(grad_attn.astype(F32), axis=0) * (1.0 / seq)
    sums_branch, sums_up = sums_mlp[0, :width] * everyone, sums_mlp[1, :hidden]
    sums_proj, sums_branch, sums_up, sums_qkv = after(
        (sums_proj, sums_branch, sums_up, sums_qkv), sent_mod
    )
    in_team = (jnp.arange(team) == me)[:, None]
    by_owner = [sums_branch.reshape(shards, rows), sums_proj.reshape(shards, rows)]
    for sums in (sums_qkv[:, :group], sums_qkv[:, 2 * group :]):
        by_owner.append(jnp.where(in_team, sums, 0.0).reshape(shards, rows))
    sums_up = link.flip(sums_up.reshape(2, high, hidden_rows), pair_bit).swapaxes(0, 1)
    sums_up = sums_up.reshape(1, rest, 1, hidden_rows)
    in_seq = jnp.arange(seq).reshape(seq, 1, 1, 1) == half
    in_core = jnp.arange(2).reshape(1, 1, 2, 1) == core
    by_owner.append(jnp.where(in_seq & in_core, sums_up, 0.0).reshape(shards, hidden_rows))
    tail = jnp.concatenate([grad_silu] + by_owner, axis=1)
    tail = lax.all_to_all(tail, AXES, 0, 0, tiled=True)
    grad_fc1 = after(keep_fc1, sums_attn).astype(F32) + sent_fc1.astype(F32)
    grad_fc1 = link.scatter(grad_fc1.astype(BF16), high_bits, (tail,), (grad_qkv,)).astype(BF16)
    grad_fc1 = link.exchange_pieces(grad_fc1.reshape(team, rows, hidden), team_bits)
    grad_fc1 = join_fc1(me, pair, grad_fc1, high)
    grad_qkv = link.scatter(grad_qkv, high_bits, (tail,))
    grad_proj = grad_qkv[:, columns:].reshape(team, rows, group)
    grad_proj = jnp.concatenate([grad_proj[at] for at in range(team)], axis=1)
    grad_qkv = grad_qkv[:, :columns].astype(BF16).reshape(team, rows, columns)
    grad_qkv = join_qkv(me, link.exchange_pieces(grad_qkv, team_bits))

    def own_rows(value):
        value = value.reshape(latents, seq_len, -1)
        return lax.dynamic_slice_in_dim(value, half * local_len, local_len, 1)

    branch = after(branch, other_attn) + sent_branch.astype(F32)
    grad_h_attn = after(grad_h_attn, sent_mod) + link.send(other_h_attn, core_bit).astype(F32)
    both = jnp.stack([branch, grad_h_attn]).reshape(2, latents, seq, local_len, width)
    both = link.scatter(jnp.moveaxis(both, 2, 0), seq_bits, (tail,))
    output = (own_rows(mid) + mod[:latents, 5:6] * both[0]).astype(BF16)
    norm, rate = norm_parts(tokens.astype(F32))
    grad_tokens = norm_back(norm, rate, both[1] * (1.0 + mod[:latents, 1:2]))
    grad_tokens = (own_rows(grad_mid) + grad_tokens).astype(BF16)

    grad_silu = tail[:, :mine].reshape(shards, latents, rows).swapaxes(0, 1)
    grad_silu = grad_silu.reshape(latents, width)
    silu_back = jax.vjp(jax.nn.silu, cond_float)[1]
    grad_cond = silu_back(grad_silu)[0].astype(BF16)
    sums = jnp.sum(tail[:, mine:], axis=0)
    return (
        output,
        grad_tokens,
        grad_cond,
        grad_ada,
        grad_b_ada,
        grad_qkv,
        sums[2 * rows : 3 * rows],
        sums[3 * rows : 4 * rows],
        grad_proj,
        sums[rows : 2 * rows],
        grad_fc1,
        sums[4 * rows :],
        grad_fc2,
        sums[:rows],
    )


def solution(mesh):
    seq, fsdp = mesh.shape["seq"], mesh.shape["fsdp"]
    act = P("fsdp", "seq", None)
    matrix = P(AXES, None)
    vector = P(AXES)
    cond = P("fsdp", None)
    in_specs = (
        act, cond, matrix, vector, matrix, vector, vector, matrix, vector, matrix, vector, matrix,
        vector, act,
    )
    out_specs = (
        act, act, cond, matrix, vector, matrix, vector, vector, matrix, vector, matrix, vector,
        matrix, vector,
    )

    def layer(*args):
        return local(seq * fsdp, (seq, fsdp), *args)

    return jax.shard_map(layer, mesh=mesh, in_specs=in_specs, out_specs=out_specs, check_vma=False)
```
